128 devices in a mesh: row: 16 (over z_hi, y, core), col: 8 (over x, z_lo).
Axes of the slice: x: 4, y: 4, z: 4 (z_hi: 2, z_lo: 2; z = z_hi * 2 + z_lo), core: 2. Of those that a mesh axis runs over, the one named last changes fastest.
Arguments:
- tile_values: bfloat16 [16, 128, 128, 128], P('row', 'col'), may hold values from 0.019897461 to 1
- tile_index: int32 [16, 128], P('row', 'col'), may hold values from -1 to 31, as said below
- keep_rows: int32 [64, 8], replicated, may hold values from 0 to 63, as said below
- slot_place: int32 [64, 8], replicated, may hold values from 0 to 63, as said below
Outputs:
- pruned: bfloat16 [8, 64, 128, 128], P('col', 'row')
The draws below stay inside these ranges and needn't reach their ends.
Inputs may be any that keep to these rules, and one draw needn't show every extreme that they name: `tile_index`: within one device's slots the non-negative entries are distinct local tile numbers (tile row * 8 + tile column); padding -1 follows them; every device lists 16 // 2 or more tiles and some device lists 16. `keep_rows`: the 8 entries of a tile column are distinct and lie in 8 different groups of 4 tile rows (entry // 4 distinct). For each block of 8 tile columns (j // 8 equal) the entries are a permutation of 0 to 63; within a block, two kept tiles whose rows share keep_rows // 4 never share slot_place // 4.
All inputs are finite; a program needn't handle non-finite values.
Results may differ from the reference program's by a relative error of at most 0.0026.
Values may be sent and summed in bfloat16 or wider, within the bound.
A program may use at most 128 MiB of HBM per device.

```python
import math
import jax
import jax.numpy as jnp

TS = 128
RT = 4
KEEP = 8
NT = 64
CT = 8
NNZ = 16
UNITS = 4
NCELLS = 8192
N_ROW = 16
N_COL = 8


def draw_tile_index(key, part):
    key = jax.random.fold_in(key, 11)
    count_dev = N_ROW * N_COL
    keys = jax.random.split(key, count_dev + 2)
    perms = jax.vmap(lambda k: jax.random.permutation(k, RT * CT)[:NNZ])(keys[:count_dev])
    counts = jax.random.randint(keys[count_dev], (count_dev,), max(NNZ // 2, 1), NNZ + 1)
    fullest = jax.random.randint(keys[count_dev + 1], (), 0, count_dev)
    counts = jnp.where(jnp.arange(count_dev) == fullest, NNZ, counts)
    entries = jnp.where(jnp.arange(NNZ)[None, :] < counts[:, None], perms, -1)
    return entries.reshape(N_ROW, N_COL * NNZ).astype(jnp.int32)


def pruning_lists(key):
    key = jax.random.fold_in(key, 51)
    key_dev, key_off = jax.random.split(key)
    keys = jax.random.split(key_dev, NT)
    devices = jax.vmap(lambda k: jax.random.permutation(k, N_ROW)[:KEEP])(keys).astype(jnp.int32)
    offsets = jax.random.randint(key_off, (NT, KEEP), 0, RT).astype(jnp.int32)
    rows = devices * RT + offsets
    source = devices.reshape(N_COL, CT * KEEP)
    order = jnp.argsort(source, axis=1, stable=True).astype(jnp.int32)
    ranks = jnp.argsort(order, axis=1, stable=True).astype(jnp.int32)
    slots = ranks % N_ROW * UNITS + ranks // N_ROW
    return (rows.astype(jnp.int32), slots.reshape(NT, KEEP).astype(jnp.int32))


def draw_keep_rows(key, part):
    rows, slots = pruning_lists(key)
    return rows


def draw_slot_place(key, part):
    rows, slots = pruning_lists(key)
    return slots


def shard_levels(stream_key, shape, cuts, low, top_value):
    def one(position, blocks):
        heights = jax.random.uniform(jax.random.fold_in(jax.random.fold_in(stream_key, 6), position), (blocks,), jnp.float32, low / len(cuts), top_value / len(cuts))
        return jnp.repeat(jnp.exp(heights), shape[position] // blocks).reshape((-1,) + (1,) * (len(shape) - position - 1))

    factor_of = one(*cuts[0])
    for cut in cuts[1:]:
        factor_of = factor_of * one(*cut)
    return factor_of


def setup_inputs(seed: int = 0) -> dict:
    key_list = jax.random.split(jax.random.key(seed), 5)
    return {
        "tile_values": jnp.clip(jnp.exp(math.log(1.0) - 3.9171631 * jax.random.uniform(key_list[0], (N_ROW, N_COL * NNZ, TS, TS), jnp.float32) ** shard_levels(key_list[0], (N_ROW, N_COL * NNZ, TS, TS), ((0, 16), (1, 8)), -0.2, 0.2)), 0.019897461, 1.0).astype(jnp.bfloat16),
        "tile_index": draw_tile_index(jax.random.fold_in(key_list[4], 71), 0),
        "keep_rows": draw_keep_rows(jax.random.fold_in(key_list[4], 71), 0),
        "slot_place": draw_slot_place(jax.random.fold_in(key_list[4], 71), 0),
    }


def reference(tile_values, tile_index, keep_rows, slot_place):
    vals = tile_values.reshape(N_ROW, N_COL, NNZ, TS, TS)
    idx = tile_index.reshape(N_ROW, N_COL, NNZ)
    safe = jnp.where(idx >= 0, idx, RT * CT).astype(jnp.int32)
    row_ids = jnp.arange(N_ROW, dtype=jnp.int32)[:, None, None]
    col_ids = jnp.arange(N_COL, dtype=jnp.int32)[None, :, None]
    tiles = jnp.zeros((N_ROW, N_COL, RT * CT + 1, TS, TS), tile_values.dtype)
    tiles = tiles.at[row_ids, col_ids, safe].set(vals)[:, :, :RT * CT]
    tiles = tiles.reshape(N_ROW, N_COL, RT, CT, TS, TS).transpose(0, 2, 4, 1, 3, 5)
    network = tiles.reshape(NCELLS, NCELLS)
    diag = jnp.arange(NCELLS, dtype=jnp.int32)
    looped = network.at[diag, diag].add(jnp.ones((NCELLS,), network.dtype))
    expanded = jnp.dot(looped, looped, preferred_element_type=jnp.float32)
    inflated = expanded * expanded
    column_total = jnp.sum(inflated, axis=0)
    normalized = (float(NCELLS) * inflated) / column_total[None, :]
    grid = normalized.reshape(NT, TS, NT, TS)
    columns = jnp.arange(NT, dtype=jnp.int32)[:, None]
    picked = grid[keep_rows, :, columns, :].astype(jnp.bfloat16)
    block = jnp.broadcast_to(columns // CT, keep_rows.shape)
    pruned = jnp.zeros((N_COL, CT * KEEP, TS, TS), jnp.bfloat16)
    return pruned.at[block, slot_place].set(picked)
```

```python
import functools

import jax
import jax.numpy as jnp
from jax import lax
from jax.experimental import pallas as pl
from jax.experimental.pallas import tpu as pltpu
from jax.sharding import PartitionSpec as P

MESH = pl.DeviceIdType.MESH
TS = 128
RT = 4
CT = 8
SLOTS = 16
HALF = SLOTS // 2
NROW = 16
NCOL = 8
KEEP = 8
UNITS = 4
NQ = 8
WIDE = 256
NW = CT * TS // WIDE
F32 = jnp.float32
I32 = jnp.int32

BEHIND, AHEAD, PARTNER, FAR, BEHIND2, AHEAD2, FAR2 = range(7)
OWN = 7
STEP = {OWN: 0, BEHIND: 1, AHEAD: 1, PARTNER: 2, FAR: 3, BEHIND2: 4, AHEAD2: 4, FAR2: 5}
N_STEPS = 6


def eye_tile():
    rows = lax.broadcasted_iota(I32, (TS, TS), 0)
    cols = lax.broadcasted_iota(I32, (TS, TS), 1)
    return jnp.where(rows == cols, 1.0, 0.0).astype(F32)


def kernel(values, index, keep, place, out, own, *scratch):
    got_a, scratch = scratch[:7], scratch[7:]
    got_b, scratch = scratch[:7], scratch[7:]
    got_s, scratch = scratch[:8], scratch[8:]
    (
        map_a, map_b, smap_a, smap_b, route, sroute,
        dense_a, dense_b, total, sums, scale, tiles_out, tiles_in,
        send_a, recv_a, send_b, recv_b, send_s, recv_s,
        msend_a, mrecv_a, msend_b, mrecv_b, ssend, srecv, tsend, trecv, local,
    ) = scratch

    r = lax.axis_index("row")
    c = lax.axis_index("col")
    core = r % 2
    ring_pos = {"a": c // 2, "b": (r // 2) % 4}
    plane = {"a": c % 2, "b": r // 8}

    def block_of(axis, pos, side):
        return pos * 2 + side if axis == "a" else side * 8 + pos * 2 + core

    def device_of(axis, pos, side):
        block = block_of(axis, pos, side)
        return (r, block) if axis == "a" else (block, c)

    sibling = (r + 1 - 2 * core, c)

    own_copy = pltpu.make_async_copy(values.at[0], own, local.at[0])
    own_copy.start()

    barrier = pltpu.get_barrier_semaphore()
    for d in range(1, NCOL):
        pl.semaphore_signal(barrier, inc=1, device_id=(r, (c + d) % NCOL), device_id_type=MESH)
    for d in range(1, NROW):
        pl.semaphore_signal(barrier, inc=1, device_id=((r + d) % NROW, c), device_id_type=MESH)

    lane = lax.broadcasted_iota(I32, (1, TS), 1)
    slot_of = jnp.full((1, TS), SLOTS, I32)
    for s in range(SLOTS):
        slot_of = jnp.where(lane == index[0, s], s, slot_of)
    map_a[0] = slot_of
    map_b[0] = slot_of

    pl.semaphore_wait(barrier, NCOL + NROW - 2)

    got = {"a": got_a, "b": got_b}
    send = {"a": send_a, "b": send_b}
    recv = {"a": recv_a, "b": recv_b}
    pending = []

    def remote(src, dst, send_sem, recv_sem, device):
        return pltpu.make_async_remote_copy(
            src_ref=src, dst_ref=dst, send_sem=send_sem, recv_sem=recv_sem, device_id=device, device_id_type=MESH
        )

    def half(ref, h):
        return ref.at[pl.ds(h * HALF, HALF)]

    def target(axis, unit, h):
        pos, side = ring_pos[axis], plane[axis]
        if unit == PARTNER:
            return device_of(axis, pos, 1 - side)
        forward = unit in (BEHIND, BEHIND2) or (unit in (FAR, FAR2) and h == 0)
        return device_of(axis, (pos + (1 if forward else 3)) % 4, side)

    def source(axis, unit, h):
        mine = got[axis]
        if unit in (BEHIND, AHEAD, PARTNER):
            return half(values.at[0], h)
        if unit in (BEHIND2, AHEAD2):
            return half(mine[PARTNER], h)
        if unit == FAR:
            return half(mine[BEHIND if h == 0 else AHEAD], h)
        return half(mine[BEHIND2 if h == 0 else AHEAD2], h)

    def bulk(axis, unit, h):
        return remote(
            source(axis, unit, h), half(got[axis][unit], h), send[axis].at[unit, h], recv[axis].at[unit, h], target(axis, unit, h)
        )

    def start(axis, unit, h):
        copy = bulk(axis, unit, h)
        copy.start()
        pending.append(copy)

    def across(unit, h):
        src = half(values.at[0], h) if unit == OWN else half(got_b[unit], h)
        return remote(src, half(got_s[unit], h), send_s.at[unit, h], recv_s.at[unit, h], sibling)

    def arrived(axis, unit, h):
        bulk(axis, unit, h).wait_recv()
        if axis == "b":
            copy = across(unit, h)
            copy.start()
            pending.append(copy)

    maps = []
    for d in range(1, NCOL):
        maps.append(remote(map_a.at[0], map_a.at[d], msend_a.at[d], mrecv_a.at[d], (r, (c + d) % NCOL)))
    for d in range(1, NROW):
        maps.append(remote(map_b.at[0], map_b.at[d], msend_b.at[d], mrecv_b.at[d], ((r + d) % NROW, c)))
    for copy in maps:
        copy.start()

    for axis in "ab":
        start(axis, BEHIND, 0)
        start(axis, AHEAD, 1)
    for axis in "ab":
        start(axis, PARTNER, 0)
    for axis in "ab":
        start(axis, BEHIND, 1)
        start(axis, AHEAD, 0)
    for axis in "ab":
        start(axis, PARTNER, 1)
    for h in range(2):
        copy = across(OWN, h)
        copy.start()
        pending.append(copy)

    def entry(e, carry):
        sending, coming = carry
        kept = keep[c * CT + e // KEEP, e % KEEP]
        slot = place[c * CT + e // KEEP, e % KEEP]
        holder, owner = kept >> 2, slot >> 2
        sending = jnp.where((lane == owner) & (holder == r), (kept & 3) * CT + e // KEEP, sending)
        coming = jnp.where((lane == (slot & 3)) & (owner == r), holder, coming)
        return sending, coming

    nothing = jnp.zeros((1, TS), I32)
    sending, coming = lax.fori_loop(0, CT * KEEP, entry, (nothing, nothing))
    route[0] = sending
    route[1] = coming
    route_copy = pltpu.make_async_copy(route, sroute, local.at[1])
    route_copy.start()

    total[...] = jnp.zeros_like(total)

    for copy in maps:
        copy.wait()
    map_copies = [
        pltpu.make_async_copy(map_a, smap_a, local.at[2]),
        pltpu.make_async_copy(map_b, smap_b, local.at[3]),
    ]
    for copy in map_copies:
        copy.start()
    for copy in map_copies:
        copy.wait()
    route_copy.wait()
    own_copy.wait()

    def tile_at(block, smap, d, l):
        s = smap[d, 0, l]
        tile = block[jnp.clip(s, 0, SLOTS - 1)]
        return jnp.where(s < SLOTS, tile, jnp.zeros_like(tile))

    def lay_a(block, q):
        d = (c + NCOL - q) % NCOL

        @pl.loop(0, RT)
        def _(lr):
            rows = pl.ds(pl.multiple_of(lr * TS, TS), TS)
            for lc in range(CT):
                dense_a[q, rows, lc * TS : (lc + 1) * TS] = tile_at(block, smap_a, d, lr * CT + lc)

    def lay_b(block, p):
        d = (r + NROW - p) % NROW
        q, upper = p // 2, p % 2

        @pl.loop(0, RT)
        def _(lr):
            rows = pl.ds(pl.multiple_of((upper * RT + lr) * TS, TS), TS)
            for lc in range(CT):
                j = lc % 2
                dense_b[q, lc // 2, rows, j * TS : (j + 1) * TS] = tile_at(block, smap_b, d, lr * CT + lc)

    def position(axis, unit):
        pos, side = ring_pos[axis], plane[axis]
        shift = {OWN: 0, BEHIND: 3, AHEAD: 1, PARTNER: 0, FAR: 2, BEHIND2: 3, AHEAD2: 1, FAR2: 2}[unit]
        other = unit in (PARTNER, BEHIND2, AHEAD2, FAR2)
        return block_of(axis, (pos + shift) % 4, 1 - side if other else side)

    def lay(unit):
        lay_a(own if unit == OWN else got_a[unit], position("a", unit))
        lay_b(own if unit == OWN else got_b[unit], position("b", unit))
        for h in range(2):
            across(unit, h).wait_recv()
        lay_b(got_s[unit], position("b", unit) + 1 - 2 * core)

    def step_of(pos, side, my_pos, my_side):
        shift = (pos + 4 - my_pos) % 4
        same = side == my_side
        first = jnp.where(same, 0, STEP[PARTNER])
        near = jnp.where(same, STEP[BEHIND], STEP[BEHIND2])
        far = jnp.where(same, STEP[FAR], STEP[FAR2])
        return jnp.where(shift == 0, first, jnp.where(shift == 2, far, near))

    def multiply(q):
        @pl.when(q == r // 2)
        def _():
            for lr in range(RT):
                cols = pl.ds(pl.multiple_of((core * RT + lr) * TS, TS), TS)
                rows = slice(lr * TS, (lr + 1) * TS)
                dense_a[q, rows, cols] = (dense_a[q, rows, cols].astype(F32) + eye_tile()).astype(jnp.bfloat16)

        @pl.when(q == c)
        def _():
            for lc in range(CT):
                j = lc % 2
                at = (q, lc // 2, slice(lc * TS, (lc + 1) * TS), slice(j * TS, (j + 1) * TS))
                dense_b[at] = (dense_b[at].astype(F32) + eye_tile()).astype(jnp.bfloat16)

        @pl.loop(0, NW)
        def _(n):
            product = jnp.dot(dense_a[q], dense_b[q, n], preferred_element_type=F32)
            for lr in range(RT):
                for j in range(WIDE // TS):
                    part = product[lr * TS : (lr + 1) * TS, j * TS : (j + 1) * TS]
                    total[lr * CT + n * (WIDE // TS) + j] += part

    def multiply_ready(step):
        @pl.loop(0, NQ)
        def _(q):
            step_a = step_of(q // 2, q % 2, ring_pos["a"], plane["a"])
            step_b = step_of(q % 4, q // 4, ring_pos["b"], plane["b"])

            @pl.when(jnp.maximum(step_a, step_b) == step)
            def _():
                multiply(q)

    lay(OWN)
    multiply_ready(0)
    for axis in "ab":
        arrived(axis, BEHIND, 0)
        start(axis, FAR, 0)
        arrived(axis, AHEAD, 1)
        start(axis, FAR, 1)
    for axis in "ab":
        arrived(axis, BEHIND, 1)
        arrived(axis, AHEAD, 0)
    lay(BEHIND)
    lay(AHEAD)
    for axis in "ab":
        arrived(axis, PARTNER, 0)
        start(axis, BEHIND2, 0)
        start(axis, AHEAD2, 0)
    multiply_ready(1)
    for axis in "ab":
        arrived(axis, PARTNER, 1)
        start(axis, AHEAD2, 1)
        start(axis, BEHIND2, 1)
    lay(PARTNER)
    multiply_ready(2)
    for axis in "ab":
        for h in range(2):
            arrived(axis, FAR, h)
    lay(FAR)
    multiply_ready(3)
    for axis in "ab":
        arrived(axis, BEHIND2, 0)
        start(axis, FAR2, 0)
    for axis in "ab":
        arrived(axis, AHEAD2, 1)
        start(axis, FAR2, 1)
    for axis in "ab":
        arrived(axis, AHEAD2, 0)
        arrived(axis, BEHIND2, 1)
    lay(BEHIND2)
    lay(AHEAD2)
    multiply_ready(4)
    for axis in "ab":
        for h in range(2):
            arrived(axis, FAR2, h)
    lay(FAR2)
    multiply_ready(5)

    for lc in range(CT):
        column = jnp.zeros((1, TS), F32)
        for lr in range(RT):
            e = total[lr * CT + lc]
            column += jnp.sum(e * e, axis=0, keepdims=True)
        sums[0, lc] = column
    shares = [
        remote(sums.at[0], sums.at[d], ssend.at[d], srecv.at[d], ((r + d) % NROW, c)) for d in range(1, NROW)
    ]
    for copy in shares:
        copy.start()
    for copy in shares:
        copy.wait()
    for lc in range(CT):
        scale[lc] = float(NROW * RT * TS) / jnp.sum(sums[:, lc], axis=0)

    moves = []
    for d in range(NROW):
        l = jnp.clip(sroute[0, 0, (r + d) % NROW], 0, RT * CT - 1)
        e = total[l]
        tile = ((e * e) * scale[l & 7]).astype(jnp.bfloat16)
        if d == 0:
            tiles_in[0] = tile
        else:
            tiles_out[d] = tile
            copy = remote(tiles_out.at[d], tiles_in.at[d], tsend.at[d], trecv.at[d], ((r + d) % NROW, c))
            copy.start()
            moves.append(copy)
    for copy in moves:
        copy.wait()
    for u in range(UNITS):
        d = (r + NROW - sroute[1, 0, u]) % NROW
        out[0, u] = tiles_in[jnp.clip(d, 0, NROW - 1)]

    for copy in pending:
        copy.wait_send()


def body(tile_values, tile_index, keep_rows, slot_place):
    bf16 = jnp.bfloat16
    block = pltpu.VMEM((SLOTS, TS, TS), bf16)
    dma = pltpu.SemaphoreType.DMA
    smem = pl.BlockSpec(memory_space=pltpu.SMEM)
    scratch = [block] * (1 + 7 + 7 + 8)
    scratch += [
        pltpu.VMEM((NCOL, 1, TS), I32),
        pltpu.VMEM((NROW, 1, TS), I32),
        pltpu.SMEM((NCOL, 1, TS), I32),
        pltpu.SMEM((NROW, 1, TS), I32),
        pltpu.VMEM((2, 1, TS), I32),
        pltpu.SMEM((2, 1, TS), I32),
        pltpu.VMEM((NQ, RT * TS, CT * TS), bf16),
        pltpu.VMEM((NQ, NW, 2 * RT * TS, WIDE), bf16),
        pltpu.VMEM((RT * CT, TS, TS), F32),
        pltpu.VMEM((NROW, CT, 1, TS), F32),
        pltpu.VMEM((CT, 1, TS), F32),
        pltpu.VMEM((NROW, TS, TS), bf16),
        pltpu.VMEM((NROW, TS, TS), bf16),
        dma((7, 2)), dma((7, 2)), dma((7, 2)), dma((7, 2)), dma((8, 2)), dma((8, 2)),
        dma((NCOL,)), dma((NCOL,)), dma((NROW,)), dma((NROW,)),
        dma((NROW,)), dma((NROW,)), dma((NROW,)), dma((NROW,)), dma((4,)),
    ]
    return pl.pallas_call(
        kernel,
        out_shape=jax.ShapeDtypeStruct((1, UNITS, TS, TS), bf16),
        in_specs=[pl.BlockSpec(memory_space=pl.ANY), smem, smem, smem],
        out_specs=pl.BlockSpec(memory_space=pltpu.VMEM),
        scratch_shapes=scratch,
        compiler_params=pltpu.CompilerParams(collective_id=0, has_side_effects=True, vmem_limit_bytes=56 * 2**20),
        cost_estimate=pl.CostEstimate(flops=2 * 512 * 8192 * 1024, bytes_accessed=2**20, transcendentals=0),
        name="clustering_step",
    )(tile_values, tile_index, keep_rows, slot_place)


def solution(mesh):
    placed = (P("row", "col", None, None), P("row", "col"), P(), P())
    return jax.shard_map(
        body, mesh=mesh, in_specs=placed, out_specs=P("col", "row", None, None), check_vma=False
    )
```

```python
import functools

import jax
import jax.numpy as jnp
from jax import lax
from jax.experimental import pallas as pl
from jax.experimental.pallas import tpu as pltpu
from jax.sharding import PartitionSpec as P

MESH = pl.DeviceIdType.MESH
TS = 128
RT = 4
CT = 8
SLOTS = 16
CHUNKS = 4
PART = SLOTS // CHUNKS
NROW = 16
NCOL = 8
KEEP = 8
UNITS = 4
NQ = 8
WIDE = 256
NW = CT * TS // WIDE
F32 = jnp.float32
I32 = jnp.int32

BEHIND, AHEAD, PARTNER, FAR, BEHIND2, AHEAD2, FAR2 = range(7)
OWN = 7
STEP = {
    "a": {OWN: 0, BEHIND: 1, AHEAD: 1, FAR: 2, PARTNER: 3, BEHIND2: 4, AHEAD2: 4, FAR2: 5},
    "b": {OWN: 0, BEHIND: 1, AHEAD: 1, FAR: 2, PARTNER: 3, BEHIND2: 4, AHEAD2: 4, FAR2: 6},
}
LAY_COST, MULTIPLY_COST = 0.15, 1.0
FROM_BEHIND = {FAR: range(CHUNKS // 2), FAR2: range(CHUNKS // 2)}
FROM_PARTNER = range(0)
ORDER_BEHIND = tuple(range(CHUNKS))
ORDER_AHEAD = tuple((k + CHUNKS // 2) % CHUNKS for k in range(CHUNKS))


def follow_ups(unit, k):
    if unit in (BEHIND, AHEAD, BEHIND2, AHEAD2):
        far = FAR if unit in (BEHIND, AHEAD) else FAR2
        if far == FAR2 and k in FROM_PARTNER:
            return []
        return [(far, k)] if (k in FROM_BEHIND[far]) == (unit in (BEHIND, BEHIND2)) else []
    if unit == PARTNER:
        return [(BEHIND2, k), (AHEAD2, k)]
    if unit == FAR and k in FROM_PARTNER:
        return [(FAR2, k)]
    return []


def link_of(unit, k):
    if unit == PARTNER or (unit == FAR2 and k in FROM_PARTNER):
        return "across"
    if unit in (FAR, FAR2):
        return "forward" if k in FROM_BEHIND[unit] else "back"
    return "forward" if unit in (BEHIND, BEHIND2) else "back"


def arrivals():
    cost = {"forward": 1.0, "back": 1.0, "across": 2.0}
    free = dict.fromkeys(cost, 0.0)
    waiting = {"forward": [(0.0, i, BEHIND, k) for i, k in enumerate(ORDER_BEHIND)]}
    waiting["back"] = [(0.0, i, AHEAD, k) for i, k in enumerate(ORDER_AHEAD)]
    waiting["across"] = [(0.0, i, PARTNER, k) for i, k in enumerate(ORDER_BEHIND)]
    done, count = [], CHUNKS
    while any(waiting.values()):
        link = min((n for n in waiting if waiting[n]), key=lambda n: (max(free[n], min(waiting[n])[0]), n))
        item = min(waiting[link], key=lambda m: (max(m[0], free[link]), m[1]))
        waiting[link].remove(item)
        ready, _, unit, k = item
        free[link] = max(free[link], ready) + cost[link]
        done.append((free[link], unit, k))
        for nxt, kk in follow_ups(unit, k):
            count += 1
            waiting[link_of(nxt, kk)].append((free[link], count, nxt, kk))
    return sorted(done, key=lambda m: m[0])


def eye_tile():
    rows = lax.broadcasted_iota(I32, (TS, TS), 0)
    cols = lax.broadcasted_iota(I32, (TS, TS), 1)
    return jnp.where(rows == cols, 1.0, 0.0).astype(F32)


def kernel(values, index_in, keep_in, place_in, out, own, *scratch):
    got_a, scratch = scratch[:7], scratch[7:]
    got_b, scratch = scratch[:7], scratch[7:]
    got_s, scratch = scratch[:8], scratch[8:]
    (
        index, keep, place,
        map_a, map_b, map_s, smap_a, smap_b, smap_s, route, sroute,
        dense_a, dense_b, total, sums, scale, tiles_out, tiles_in,
        send_a, recv_a, send_b, recv_b, send_s, recv_s,
        msend_a, mrecv_a, msend_b, mrecv_b, msend_s, mrecv_s, mlocal_a, mlocal_b, mlocal_s,
        ssend, srecv, tsend, trecv, local,
    ) = scratch

    r = lax.axis_index("row")
    c = lax.axis_index("col")
    core = r % 2
    ring_pos = {"a": c // 2, "b": (r // 2) % 4}
    plane = {"a": c % 2, "b": r // 8}

    def block_of(axis, pos, side):
        return pos * 2 + side if axis == "a" else side * 8 + pos * 2 + core

    def device_of(axis, pos, side):
        block = block_of(axis, pos, side)
        return (r, block) if axis == "a" else (block, c)

    sibling = (r + 1 - 2 * core, c)

    index_copy = pltpu.make_async_copy(index_in, index, local.at[2])
    index_copy.start()
    own_copy = pltpu.make_async_copy(values.at[0], own, local.at[0])
    own_copy.start()

    barrier = pltpu.get_barrier_semaphore()
    neighbours = [sibling]
    for axis in "ab":
        pos, side = ring_pos[axis], plane[axis]
        neighbours += [device_of(axis, (pos + 1) % 4, side), device_of(axis, (pos + 3) % 4, side), device_of(axis, pos, 1 - side)]
    for device in neighbours:
        pl.semaphore_signal(barrier, inc=1, device_id=device, device_id_type=MESH)
    pl.semaphore_wait(barrier, len(neighbours))

    got = {"a": got_a, "b": got_b}
    send = {"a": send_a, "b": send_b}
    recv = {"a": recv_a, "b": recv_b}
    maps = {"a": map_a, "b": map_b}
    smaps = {"a": smap_a, "b": smap_b, "s": smap_s}
    msend = {"a": msend_a, "b": msend_b}
    mrecv = {"a": mrecv_a, "b": mrecv_b}
    mlocal = {"a": mlocal_a, "b": mlocal_b, "s": mlocal_s}
    pending = []

    def remote(src, dst, send_sem, recv_sem, device):
        return pltpu.make_async_remote_copy(
            src_ref=src, dst_ref=dst, send_sem=send_sem, recv_sem=recv_sem, device_id=device, device_id_type=MESH
        )

    def part(ref, k):
        return ref.at[pl.ds(k * PART, PART)]

    def target(axis, unit, k):
        pos, side = ring_pos[axis], plane[axis]
        link = link_of(unit, k)
        if link == "across":
            return device_of(axis, pos, 1 - side)
        return device_of(axis, (pos + (1 if link == "forward" else 3)) % 4, side)

    def source(axis, unit, k):
        mine = got[axis]
        if unit in (BEHIND, AHEAD, PARTNER):
            return part(values.at[0], k)
        if unit in (BEHIND2, AHEAD2):
            return part(mine[PARTNER], k)
        if unit == FAR2 and k in FROM_PARTNER:
            return part(mine[FAR], k)
        near = (BEHIND, AHEAD) if unit == FAR else (BEHIND2, AHEAD2)
        return part(mine[near[0] if k in FROM_BEHIND[unit] else near[1]], k)

    def bulk(axis, unit, k):
        return remote(
            source(axis, unit, k), part(got[axis][unit], k), send[axis].at[unit, k], recv[axis].at[unit, k], target(axis, unit, k)
        )

    def start(axis, unit, k):
        start_all(bulk(axis, unit, k))

    def across(unit, k):
        src = part(values.at[0], k) if unit == OWN else part(got_b[unit], k)
        return remote(src, part(got_s[unit], k), send_s.at[unit, k], recv_s.at[unit, k], sibling)

    def start_across(unit, k):
        start_all(across(unit, k))

    def map_copy(axis, unit):
        first = {BEHIND: OWN, AHEAD: OWN, PARTNER: OWN, BEHIND2: PARTNER, AHEAD2: PARTNER, FAR: BEHIND, FAR2: BEHIND2}[unit]
        k = 0 if unit in (FAR, FAR2) else ORDER_BEHIND[0]
        ref = maps[axis]
        return remote(ref.at[first], ref.at[unit], msend[axis].at[unit], mrecv[axis].at[unit], target(axis, unit, k))

    def map_across(unit):
        return remote(map_b.at[unit], map_s.at[unit], msend_s.at[unit], mrecv_s.at[unit], sibling)

    def map_inward(axis, unit):
        ref = map_s if axis == "s" else maps[axis]
        return pltpu.make_async_copy(ref.at[unit], smaps[axis].at[unit], mlocal[axis].at[unit])

    def start_all(*copies):
        for copy in copies:
            copy.start()
            pending.append(copy)

    def pass_map(axis, unit):
        map_copy(axis, unit).wait_recv()
        onward = {BEHIND: [FAR], PARTNER: [BEHIND2, AHEAD2], BEHIND2: [FAR2]}.get(unit, [])
        start_all(*[map_copy(axis, nxt) for nxt in onward])
        map_inward(axis, unit).start()
        if axis == "b":
            start_all(map_across(unit))

    def start_own(i):
        for axis in "ab":
            start(axis, BEHIND, ORDER_BEHIND[i])
            start(axis, AHEAD, ORDER_AHEAD[i])
        for axis in "ab":
            start(axis, PARTNER, ORDER_BEHIND[i])

    start_own(0)
    index_copy.wait()
    lane = lax.broadcasted_iota(I32, (1, TS), 1)
    slot_of = jnp.full((1, TS), SLOTS, I32)
    for s in range(SLOTS):
        slot_of = jnp.where(lane == index[0, s], s, slot_of)
    map_a[OWN] = slot_of
    map_b[OWN] = slot_of

    for axis in "ab":
        start_all(*[map_copy(axis, unit) for unit in (BEHIND, AHEAD, PARTNER)])
        map_inward(axis, OWN).start()
    start_all(map_across(OWN))
    for i in range(1, CHUNKS):
        start_own(i)
    for k in range(CHUNKS):
        start_across(OWN, k)
    list_copies = [pltpu.make_async_copy(keep_in, keep, local.at[3]), pltpu.make_async_copy(place_in, place, local.at[4])]
    for copy in list_copies:
        copy.start()

    total[...] = jnp.zeros_like(total)
    for copy in list_copies:
        copy.wait()

    def entry(e, carry):
        sending, coming = carry
        kept = keep[e % KEEP, c * CT + e // KEEP]
        slot = place[e % KEEP, c * CT + e // KEEP]
        holder, owner = kept >> 2, slot >> 2
        sending = jnp.where((lane == owner) & (holder == r), (kept & 3) * CT + e // KEEP, sending)
        coming = jnp.where((lane == (slot & 3)) & (owner == r), holder * CT + e // KEEP, coming)
        return sending, coming

    nothing = jnp.zeros((1, TS), I32)
    sending, coming = lax.fori_loop(0, CT * KEEP, entry, (nothing, nothing))
    route[0] = sending
    route[1] = coming
    route_copy = pltpu.make_async_copy(route, sroute, local.at[1])
    route_copy.start()
    own_copy.wait()

    def tile_at(block, smap, unit, l):
        s = smap[unit, 0, l]
        tile = block[jnp.clip(s, 0, SLOTS - 1)]
        return jnp.where(s < SLOTS, tile, jnp.zeros_like(tile))

    def lay_a(block, smap, unit, q):
        @pl.loop(0, RT)
        def _(lr):
            rows = pl.ds(pl.multiple_of(lr * TS, TS), TS)
            for lc in range(CT):
                dense_a[q, rows, lc * TS : (lc + 1) * TS] = tile_at(block, smap, unit, lr * CT + lc)

    def lay_b(block, smap, unit, p):
        q, upper = p // 2, p % 2

        @pl.loop(0, RT)
        def _(lr):
            rows = pl.ds(pl.multiple_of((upper * RT + lr) * TS, TS), TS)
            for lc in range(CT):
                j = lc % 2
                dense_b[q, lc // 2, rows, j * TS : (j + 1) * TS] = tile_at(block, smap, unit, lr * CT + lc)

    def position(axis, unit):
        pos, side = ring_pos[axis], plane[axis]
        shift = {OWN: 0, BEHIND: 3, AHEAD: 1, PARTNER: 0, FAR: 2, BEHIND2: 3, AHEAD2: 1, FAR2: 2}[unit]
        other = unit in (PARTNER, BEHIND2, AHEAD2, FAR2)
        return block_of(axis, (pos + shift) % 4, 1 - side if other else side)

    def lay(which, unit):
        if which == "s":
            for k in range(CHUNKS):
                across(unit, k).wait_recv()
            map_across(unit).wait_recv()
            inward = map_inward("s", unit)
            inward.start()
            inward.wait()
            lay_b(got_s[unit], smap_s, unit, position("b", unit) + 1 - 2 * core)
            return
        block = own if unit == OWN else got[which][unit]
        map_inward(which, unit).wait()
        (lay_a if which == "a" else lay_b)(block, smaps[which], unit, position(which, unit))

    def step_of(axis, pos, side):
        steps = STEP[axis]
        shift = (pos + 4 - ring_pos[axis]) % 4
        same = side == plane[axis]
        first = jnp.where(same, steps[OWN], steps[PARTNER])
        near = jnp.where(same, steps[BEHIND], steps[BEHIND2])
        far = jnp.where(same, steps[FAR], steps[FAR2])
        return jnp.where(shift == 0, first, jnp.where(shift == 2, far, near))

    def add_eyes(q):
        @pl.when(q == r // 2)
        def _():
            for lr in range(RT):
                cols = pl.ds(pl.multiple_of((core * RT + lr) * TS, TS), TS)
                rows = slice(lr * TS, (lr + 1) * TS)
                dense_a[q, rows, cols] = (dense_a[q, rows, cols].astype(F32) + eye_tile()).astype(jnp.bfloat16)

        @pl.when(q == c)
        def _():
            for lc in range(CT):
                j = lc % 2
                at = (q, lc // 2, slice(lc * TS, (lc + 1) * TS), slice(j * TS, (j + 1) * TS))
                dense_b[at] = (dense_b[at].astype(F32) + eye_tile()).astype(jnp.bfloat16)

    def multiply(q, ns):
        if 0 in ns:
            add_eyes(q)
        for n in ns:
            product = jnp.dot(dense_a[q], dense_b[q, n], preferred_element_type=F32)
            for lr in range(RT):
                for j in range(WIDE // TS):
                    part = product[lr * TS : (lr + 1) * TS, j * TS : (j + 1) * TS]
                    total[lr * CT + n * (WIDE // TS) + j] += part

    def multiply_ready(step, ns):
        @pl.loop(0, NQ)
        def _(q):
            needs = jnp.maximum(step_of("a", q // 2, q % 2), step_of("b", q % 4, q // 4))

            @pl.when(needs == step)
            def _():
                multiply(q, ns)

    work = [("lay", w, OWN) for w in "abs"] + [("multiply", 0, range(NW))]
    for step in range(1, max(STEP["b"].values()) + 1):
        for unit in sorted(STEP["a"]):
            if STEP["a"][unit] == step:
                work.append(("lay", "a", unit))
        for unit in sorted(STEP["b"]):
            if STEP["b"][unit] == step:
                work += [("lay", "b", unit), ("lay", "s", unit)]
        if step < 5:
            work += [("multiply", step, range(NW // 2)), ("multiply", step, range(NW // 2, NW))]
        else:
            work.append(("multiply", step, range(NW)))
    missing = {unit: CHUNKS for unit in range(OWN)}
    missing[OWN] = 0

    def work_on(budget):
        while work and budget > 0:
            kind, which, what = work[0]
            if kind == "lay" and missing[what]:
                return 0.0
            work.pop(0)
            if kind == "lay":
                lay(which, what)
                budget -= LAY_COST
            else:
                multiply_ready(which, what)
                budget -= MULTIPLY_COST * len(what) / NW
        return budget

    budget, last = 0.5, 0.0
    for when, unit, k in arrivals():
        budget = work_on(budget + when - last)
        last = when
        for axis in "ab":
            bulk(axis, unit, k).wait_recv()
            start_all(*[bulk(axis, nxt, kk) for nxt, kk in follow_ups(unit, k)])
            if axis == "b":
                start_all(across(unit, k))
        missing[unit] -= 1
        if missing[unit] == (CHUNKS - 2 if unit in (BEHIND, PARTNER, BEHIND2) else 0):
            for axis in "ab":
                pass_map(axis, unit)
    work_on(1e9)

    for lc in range(CT):
        column = jnp.zeros((1, TS), F32)
        for lr in range(RT):
            e = total[lr * CT + lc]
            column += jnp.sum(e * e, axis=0, keepdims=True)
        sums[0, lc] = column
    shares = [
        remote(sums.at[0], sums.at[d], ssend.at[d], srecv.at[d], ((r + d) % NROW, c)) for d in range(1, NROW)
    ]
    for copy in shares:
        copy.start()
    for copy in shares:
        copy.wait()
    for lc in range(CT):
        scale[lc] = float(NROW * RT * TS) / jnp.sum(sums[:, lc], axis=0)

    route_copy.wait()
    moves = []
    for d in range(NROW):
        l = jnp.clip(sroute[0, 0, (r + d) % NROW], 0, RT * CT - 1)
        e = total[l]
        tile = ((e * e) * scale[l & 7]).astype(jnp.bfloat16)
        if d == 0:
            tiles_in[0] = tile
        else:
            tiles_out[d] = tile
            copy = remote(tiles_out.at[d], tiles_in.at[d], tsend.at[d], trecv.at[d], ((r + d) % NROW, c))
            copy.start()
            moves.append(copy)
    for copy in pending:
        copy.wait_send()
    for copy in moves:
        copy.wait()
    for u in range(UNITS):
        d = (r + NROW - (sroute[1, 0, u] >> 3)) % NROW
        out[0, u] = tiles_in[jnp.clip(d, 0, NROW - 1)]


def body(tile_values, tile_index, keep_rows, slot_place):
    bf16 = jnp.bfloat16
    block = pltpu.VMEM((SLOTS, TS, TS), bf16)
    dma = pltpu.SemaphoreType.DMA
    place = pl.BlockSpec(memory_space=pl.ANY)
    scratch = [block] * (1 + 7 + 7 + 8)
    scratch += [
        pltpu.SMEM((1, SLOTS), I32),
        pltpu.SMEM((KEEP, 64), I32),
        pltpu.SMEM((KEEP, 64), I32),
        pltpu.VMEM((8, 1, TS), I32),
        pltpu.VMEM((8, 1, TS), I32),
        pltpu.VMEM((8, 1, TS), I32),
        pltpu.SMEM((8, 1, TS), I32),
        pltpu.SMEM((8, 1, TS), I32),
        pltpu.SMEM((8, 1, TS), I32),
        pltpu.VMEM((2, 1, TS), I32),
        pltpu.SMEM((2, 1, TS), I32),
        pltpu.VMEM((NQ, RT * TS, CT * TS), bf16),
        pltpu.VMEM((NQ, NW, 2 * RT * TS, WIDE), bf16),
        pltpu.VMEM((RT * CT, TS, TS), F32),
        pltpu.VMEM((NROW, CT, 1, TS), F32),
        pltpu.VMEM((CT, 1, TS), F32),
        pltpu.VMEM((NROW, TS, TS), bf16),
        pltpu.VMEM((NROW, TS, TS), bf16),
        dma((7, CHUNKS)), dma((7, CHUNKS)), dma((7, CHUNKS)), dma((7, CHUNKS)), dma((8, CHUNKS)), dma((8, CHUNKS)),
        *[dma((8,))] * 9,
        dma((NROW,)), dma((NROW,)), dma((NROW,)), dma((NROW,)), dma((5,)),
    ]
    return pl.pallas_call(
        kernel,
        out_shape=jax.ShapeDtypeStruct((1, UNITS, TS, TS), bf16),
        in_specs=[place] * 4,
        out_specs=pl.BlockSpec(memory_space=pltpu.VMEM),
        scratch_shapes=scratch,
        compiler_params=pltpu.CompilerParams(collective_id=0, has_side_effects=True, vmem_limit_bytes=56 * 2**20),
        cost_estimate=pl.CostEstimate(flops=2 * 512 * 8192 * 1024, bytes_accessed=2**20, transcendentals=0),
        name="clustering_step",
    )(tile_values, tile_index, keep_rows.T, slot_place.T)


def solution(mesh):
    placed = (P("row", "col", None, None), P("row", "col"), P(), P())
    return jax.shard_map(
        body, mesh=mesh, in_specs=placed, out_specs=P("col", "row", None, None), check_vma=False
    )
```

```python
import jax
import jax.numpy as jnp
from jax import lax
from jax.experimental import pallas as pl
from jax.experimental.pallas import tpu as pltpu
from jax.sharding import PartitionSpec as P

MESH = pl.DeviceIdType.MESH
TS = 128
RT = 4
CT = 8
SLOTS = 16
NROW = 16
NCOL = 8
KEEP = 8
UNITS = 4
NQ = 8
WIDE = 256
NW = CT * TS // WIDE
BATCH = 4
LEVELS = 32767.0
F32 = jnp.float32
I32 = jnp.int32
BF16 = jnp.bfloat16

BEHIND, AHEAD, PARTNER, FAR, BEHIND2, AHEAD2, FAR2, OWN = range(8)
NEAR_PIECES = {
    "+": [(0, 4, "+"), (4, 4, "+"), (8, 4, "+"), (12, 4, "+")],
    "-": [(8, 4, "-"), (12, 4, "-"), (0, 4, "-"), (4, 4, "-")],
    "z": [(0, 4, "z"), (12, 4, "z"), (4, 4, "z"), (8, 4, "z")],
}
FAR_PIECES = [(0, 4, "+"), (4, 4, "+"), (8, 4, "-"), (12, 4, "-")]
FAR2_PIECES = {
    "a": [(0, 4, "+"), (4, 2, "+"), (6, 2, "z"), (8, 2, "z"), (10, 2, "-"), (12, 4, "-")],
    "b": [(0, 4, "+"), (4, 4, "z"), (8, 4, "z"), (12, 4, "-")],
}
PIECES = {
    axis: {
        BEHIND: NEAR_PIECES["+"], AHEAD: NEAR_PIECES["-"], PARTNER: NEAR_PIECES["z"], FAR: FAR_PIECES,
        BEHIND2: [(s, n, "+") for s, n, _ in NEAR_PIECES["z"]], AHEAD2: [(s, n, "-") for s, n, _ in NEAR_PIECES["z"]],
        FAR2: FAR2_PIECES[axis], OWN: [(0, 4, ""), (4, 4, ""), (8, 4, ""), (12, 4, "")],
    }
    for axis in "ab"
}
MOST = 6
HELD = {axis: {(FAR2, k) for k, p in enumerate(PIECES[axis][FAR2]) if p[2] != "z"} for axis in "ab"}
STEP = {
    "a": {OWN: 0, BEHIND: 1, AHEAD: 1, FAR: 2, PARTNER: 3, BEHIND2: 4, AHEAD2: 4, FAR2: 5},
    "b": {OWN: 0, BEHIND: 1, AHEAD: 1, FAR: 2, PARTNER: 3, BEHIND2: 4, AHEAD2: 4, FAR2: 6},
}
SLICES = {0: 1, 4: 1, 5: 1, 6: 1, 7: 1, 8: 1, 9: 2, 10: 2, 11: 2}


def origin(unit, way):
    if unit in (BEHIND, AHEAD, PARTNER):
        return OWN
    if unit in (BEHIND2, AHEAD2):
        return PARTNER
    if unit == FAR:
        return BEHIND if way == "+" else AHEAD
    return {"+": BEHIND2, "-": AHEAD2, "z": FAR}[way]


def follow_ups(axis, unit, i):
    first, count, _ = PIECES[axis][unit][i]
    found = []
    for nxt in (FAR, BEHIND2, AHEAD2, FAR2):
        for k, (s, n, way) in enumerate(PIECES[axis][nxt]):
            if origin(nxt, way) == unit and first <= s and s + n <= first + count:
                found.append((nxt, k))
    return found


def arrivals():
    free, waiting, done = {}, {}, []
    for axis in "ba":
        for unit in (PARTNER, BEHIND, AHEAD):
            for i, (_, n, way) in enumerate(PIECES[axis][unit]):
                link = way if way == "z" else axis + way
                waiting.setdefault(link, []).append((0.0, i, axis, unit, i, n / 4))
                free[link] = 0.0
    count, held, partner = 100, {"a": [], "b": []}, {"a": 4, "b": 4}
    while any(waiting.values()):
        link = min((n for n in waiting if waiting[n]), key=lambda n: (max(free[n], min(waiting[n])[0]), n))
        item = min(waiting[link], key=lambda m: (max(m[0], free[link]), m[1], m[2]))
        waiting[link].remove(item)
        ready, _, axis, unit, i, cost = item
        free[link] = max(free[link], ready) + cost
        partner[axis] -= unit == PARTNER
        sends = follow_ups(axis, unit, i)
        if partner[axis]:
            held[axis] += [m for m in sends if m in HELD[axis]]
            sends = [m for m in sends if m not in HELD[axis]]
        elif held[axis]:
            sends += sorted(held[axis])
            held[axis] = []
        done.append((free[link], axis, unit, i, sends))
        for nxt, k in sends:
            count += 1
            _, n, way = PIECES[axis][nxt][k]
            waiting[way if way == "z" else axis + way].append((free[link], count, axis, nxt, k, n / 4))
    return sorted(done, key=lambda m: m[0])


def eye_tile():
    rows = lax.broadcasted_iota(I32, (TS, TS), 0)
    cols = lax.broadcasted_iota(I32, (TS, TS), 1)
    return jnp.where(rows == cols, 1.0, 0.0).astype(F32)


def kernel(values, index_in, keep_in, place_in, out, own, *scratch):
    got_a, scratch = scratch[:7], scratch[7:]
    got_b, scratch = scratch[:7], scratch[7:]
    got_s, scratch = scratch[:8], scratch[8:]
    (
        index, keep, place,
        map_a, map_b, map_s, smap_a, smap_b, smap_s, route, sroute,
        dense_a, dense_b, total, sums_out, sums_in, scale, tiles_out, tiles_in,
        send_a, recv_a, send_b, recv_b, send_s, recv_s,
        msend_a, mrecv_a, msend_b, mrecv_b, msend_s, mrecv_s, mlocal_a, mlocal_b, mlocal_s,
        ssend, srecv, tsend, trecv, local,
    ) = scratch

    r = lax.axis_index("row")
    c = lax.axis_index("col")
    core = r % 2
    ring_pos = {"a": c // 2, "b": (r // 2) % 4}
    plane = {"a": c % 2, "b": r // 8}
    got = {"a": got_a, "b": got_b}
    send = {"a": send_a, "b": send_b}
    recv = {"a": recv_a, "b": recv_b}
    maps = {"a": map_a, "b": map_b, "s": map_s}
    smaps = {"a": smap_a, "b": smap_b, "s": smap_s}
    msend = {"a": msend_a, "b": msend_b}
    mrecv = {"a": mrecv_a, "b": mrecv_b}
    mlocal = {"a": mlocal_a, "b": mlocal_b, "s": mlocal_s}
    pending = []

    def block_of(axis, pos, side):
        return pos * 2 + side if axis == "a" else side * 8 + pos * 2 + core

    def device_of(axis, pos, side):
        block = block_of(axis, pos, side)
        return (r, block) if axis == "a" else (block, c)

    def towards(axis, way):
        pos, side = ring_pos[axis], plane[axis]
        if way == "z":
            return device_of(axis, pos, 1 - side)
        return device_of(axis, (pos + (1 if way == "+" else 3)) % 4, side)

    sibling = (r + 1 - 2 * core, c)

    index_copy = pltpu.make_async_copy(index_in, index, local.at[2])
    index_copy.start()
    own_copy = pltpu.make_async_copy(values.at[0], own.at[pl.ds(0, SLOTS)], local.at[0])
    own_copy.start()

    barrier = pltpu.get_barrier_semaphore()
    neighbours = [sibling] + [towards(axis, way) for axis in "ab" for way in "+-z"]
    for device in neighbours:
        pl.semaphore_signal(barrier, inc=1, device_id=device, device_id_type=MESH)
    pl.semaphore_wait(barrier, len(neighbours))

    def remote(src, dst, send_sem, recv_sem, device):
        return pltpu.make_async_remote_copy(
            src_ref=src, dst_ref=dst, send_sem=send_sem, recv_sem=recv_sem, device_id=device, device_id_type=MESH
        )

    def part(ref, piece):
        return ref.at[pl.ds(piece[0], piece[1])]

    def bulk(axis, unit, i):
        piece = PIECES[axis][unit][i]
        source = origin(unit, piece[2])
        src = values.at[0] if source == OWN else got[axis][source]
        return remote(
            part(src, piece), part(got[axis][unit], piece), send[axis].at[unit, i], recv[axis].at[unit, i], towards(axis, piece[2])
        )

    def across(unit, i):
        piece = PIECES["b"][unit][i]
        src = values.at[0] if unit == OWN else got_b[unit]
        return remote(part(src, piece), part(got_s[unit], piece), send_s.at[unit, i], recv_s.at[unit, i], sibling)

    def map_copy(axis, unit):
        way = "z" if unit == PARTNER else "-" if unit in (AHEAD, AHEAD2) else "+"
        ref = maps[axis]
        return remote(ref.at[origin(unit, way)], ref.at[unit], msend[axis].at[unit], mrecv[axis].at[unit], towards(axis, way))

    def map_across(unit):
        return remote(map_b.at[unit], map_s.at[unit], msend_s.at[unit], mrecv_s.at[unit], sibling)

    def map_inward(axis, unit):
        return pltpu.make_async_copy(maps[axis].at[unit], smaps[axis].at[unit], mlocal[axis].at[unit])

    def start_all(*copies):
        for make, *args in copies:
            make(*args).start()
            pending.append((make, *args))

    def pass_map(axis, unit):
        map_copy(axis, unit).wait_recv()
        onward = {BEHIND: [FAR], PARTNER: [BEHIND2, AHEAD2], BEHIND2: [FAR2]}.get(unit, [])
        start_all(*[(map_copy, axis, nxt) for nxt in onward])
        map_inward(axis, unit).start()
        if axis == "b":
            start_all((map_across, unit))

    def start_own(i):
        for axis in "ba":
            start_all((bulk, axis, PARTNER, i))
        for axis in "ba":
            start_all((bulk, axis, BEHIND, i), (bulk, axis, AHEAD, i))

    start_own(0)
    index_copy.wait()
    lane = lax.broadcasted_iota(I32, (1, TS), 1)
    slot_of = jnp.full((1, TS), SLOTS, I32)
    for s in range(SLOTS):
        slot_of = jnp.where(lane == index[0, s], s, slot_of)
    map_a[OWN] = slot_of
    map_b[OWN] = slot_of
    for axis in "ab":
        start_all(*[(map_copy, axis, unit) for unit in (BEHIND, AHEAD, PARTNER)])
        map_inward(axis, OWN).start()
    start_all((map_across, OWN))
    for i in range(1, 4):
        start_own(i)
    for i in range(4):
        start_all((across, OWN, i))
    list_copies = [pltpu.make_async_copy(keep_in, keep, local.at[3]), pltpu.make_async_copy(place_in, place, local.at[4])]
    for copy in list_copies:
        copy.start()

    total[...] = jnp.zeros_like(total)
    for block in (own, *got_a, *got_b, *got_s):
        block[SLOTS] = jnp.zeros((TS, TS), BF16)
    for copy in list_copies:
        copy.wait()

    def entry(e, carry):
        sending, coming = carry
        kept = keep[e % KEEP, c * CT + e // KEEP]
        slot = place[e % KEEP, c * CT + e // KEEP]
        holder, owner = kept >> 2, slot >> 2
        sending = jnp.where((lane == owner) & (holder == r), (kept & 3) * CT + e // KEEP, sending)
        coming = jnp.where((lane == (slot & 3)) & (owner == r), holder * CT + e // KEEP, coming)
        return sending, coming

    nothing = jnp.zeros((1, TS), I32)
    sending, coming = lax.fori_loop(0, CT * KEEP, entry, (nothing, nothing))
    route[0] = sending
    route[1] = coming
    route_copy = pltpu.make_async_copy(route, sroute, local.at[1])
    route_copy.start()
    own_copy.wait()

    def lay_rows(block, smap, unit, store):
        @pl.loop(0, RT)
        def _(lr):
            for first in range(0, CT, BATCH):
                some = range(first, first + BATCH)
                tiles = [block[smap[unit, 0, lr * CT + lc]] for lc in some]
                for lc, tile in zip(some, tiles):
                    store(lr, lc, tile)

    def lay_a(block, smap, unit, q):
        def store(lr, lc, tile):
            rows = pl.ds(pl.multiple_of(lr * TS, TS), TS)
            dense_a[q, rows, lc * TS : (lc + 1) * TS] = tile

        lay_rows(block, smap, unit, store)

    def lay_b(block, smap, unit, p):
        q, upper = p // 2, p % 2

        def store(lr, lc, tile):
            rows = pl.ds(pl.multiple_of((upper * RT + lr) * TS, TS), TS)
            j = lc % 2
            dense_b[q, lc // 2, rows, j * TS : (j + 1) * TS] = tile

        lay_rows(block, smap, unit, store)

    def position(axis, unit):
        pos, side = ring_pos[axis], plane[axis]
        shift = {OWN: 0, BEHIND: 3, AHEAD: 1, PARTNER: 0, FAR: 2, BEHIND2: 3, AHEAD2: 1, FAR2: 2}[unit]
        other = unit in (PARTNER, BEHIND2, AHEAD2, FAR2)
        return block_of(axis, (pos + shift) % 4, 1 - side if other else side)

    def lay(which, unit):
        if which == "s":
            for i in range(len(PIECES["b"][unit])):
                across(unit, i).wait_recv()
            map_across(unit).wait_recv()
            inward = map_inward("s", unit)
            inward.start()
            inward.wait()
            lay_b(got_s[unit], smap_s, unit, position("b", unit) + 1 - 2 * core)
            return
        block = own if unit == OWN else got[which][unit]
        map_inward(which, unit).wait()
        (lay_a if which == "a" else lay_b)(block, smaps[which], unit, position(which, unit))

    def step_of(axis, pos, side):
        steps = STEP[axis]
        shift = (pos + 4 - ring_pos[axis]) % 4
        same = side == plane[axis]
        first = jnp.where(same, steps[OWN], steps[PARTNER])
        near = jnp.where(same, steps[BEHIND], steps[BEHIND2])
        far = jnp.where(same, steps[FAR], steps[FAR2])
        return jnp.where(shift == 0, first, jnp.where(shift == 2, far, near))

    def add_eyes(q):
        @pl.when(q == r // 2)
        def _():
            for lr in range(RT):
                cols = pl.ds(pl.multiple_of((core * RT + lr) * TS, TS), TS)
                rows = slice(lr * TS, (lr + 1) * TS)
                dense_a[q, rows, cols] = (dense_a[q, rows, cols].astype(F32) + eye_tile()).astype(BF16)

        @pl.when(q == c)
        def _():
            for lc in range(CT):
                j = lc % 2
                at = (q, lc // 2, slice(lc * TS, (lc + 1) * TS), slice(j * TS, (j + 1) * TS))
                dense_b[at] = (dense_b[at].astype(F32) + eye_tile()).astype(BF16)

    def multiply(q):
        add_eyes(q)
        for n in range(NW):
            product = jnp.dot(dense_a[q], dense_b[q, n], preferred_element_type=F32)
            for lr in range(RT):
                for j in range(WIDE // TS):
                    tile = product[lr * TS : (lr + 1) * TS, j * TS : (j + 1) * TS]
                    total[lr * CT + n * (WIDE // TS) + j] += tile

    events = arrivals()
    missing = {(axis, unit): len(PIECES[axis][unit]) for axis in "ab" for unit in range(OWN)}
    for axis in "ab":
        missing[axis, OWN] = 0
    left = [(axis, unit) for step in range(7) for axis in "ab" for unit in STEP[axis] if STEP[axis][unit] == step]
    phases = []
    for when in sorted({0.0} | {event[0] for event in events}):
        now = [event for event in events if event[0] == when]
        for _, axis, unit, _, _ in now:
            missing[axis, unit] -= 1
        lays = []
        while left and not missing[left[0]] and left[0] != ("b", FAR2):
            lays.append(left.pop(0))
        step = max(-1, min([STEP[axis][unit] for axis, unit in left]) - 1)
        if when % 1 and when < 11:
            carried = now
            phases.append([carried, lays, step, 0])
        else:
            phases.append([now, lays, step, SLICES.get(when, 8 if when > 11 else 0)])
    phases.append([[], left, 6, 8])
    merged = []
    for phase in phases:
        if merged and merged[-1][3] == 0:
            before = merged.pop()
            phase = [before[0] + phase[0], before[1] + phase[1], phase[2], phase[3]]
        merged.append(phase)
    phases = merged
    counts = {(axis, unit): len(PIECES[axis][unit]) for axis in "ab" for unit in range(OWN)}

    needs = [jnp.maximum(step_of("a", q // 2, q % 2), step_of("b", q % 4, q // 4)) for q in range(NQ)]
    places = []

    def total_of(terms):
        return sum(terms[1:], terms[0])

    for q in range(NQ):
        before = [(needs[p] <= needs[q] if p < q else needs[p] < needs[q]).astype(I32) for p in range(NQ) if p != q]
        places.append(total_of(before))

    def phase_work(phase):
        for _, axis, unit, k, sends in phase[0]:
            bulk(axis, unit, k).wait_recv()
            start_all(*[(bulk, axis, nxt, kk) for nxt, kk in sends])
            if axis == "b":
                start_all((across, unit, k))
            counts[axis, unit] -= 1
            if counts[axis, unit] == (2 if unit in (BEHIND, PARTNER, BEHIND2) else 0):
                pass_map(axis, unit)
        for axis, unit in phase[1]:
            lay(axis, unit)
            if axis == "b":
                lay("s", unit)

    def one_phase(t, done):
        for i, phase in enumerate(phases):
            pl.when(t == i)(lambda phase=phase: phase_work(phase))
        upto = total_of([(t == i).astype(I32) * phase[2] for i, phase in enumerate(phases)])
        most = total_of([(t == i).astype(I32) * phase[3] for i, phase in enumerate(phases)])
        ready = total_of([(n <= upto).astype(I32) for n in needs])
        until = jnp.maximum(done, jnp.minimum(done + most, ready))

        def one_slice(j, carry):
            q = total_of([(p == j).astype(I32) * i for i, p in enumerate(places)])
            multiply(q)
            return carry

        lax.fori_loop(done, until, one_slice, 0)
        return until

    lax.fori_loop(0, len(phases), one_phase, r * 0)

    route_copy.wait()

    def coded(d):
        e = total[jnp.clip(sroute[0, 0, (r + d) % NROW], 0, RT * CT - 1)]
        top = jnp.max(jnp.abs(e), axis=0, keepdims=True)
        steps_per = jnp.where(top > 0, LEVELS / top, 0.0)
        return jnp.floor(e * steps_per + 0.5).astype(I32).astype(jnp.int16), top

    def tile_move(d):
        return remote(tiles_out.at[d], tiles_in.at[d], tsend.at[d], trecv.at[d], ((r + d) % NROW, c))

    def sums_move(d):
        return remote(sums_out.at[d], sums_in.at[d], ssend.at[d], srecv.at[d], ((r + d) % NROW, c))

    @pl.loop(0, NROW - 1)
    def _(i):
        d = NROW // 2 + (i % 2) * ((i + 1) // 2) - (1 - i % 2) * (i // 2)
        tiles_out[d], sums_out[d, CT] = coded(d)
        tile_move(d).start()

    for lc in range(CT):
        column = jnp.zeros((1, TS), F32)
        for lr in range(RT):
            e = total[lr * CT + lc]
            column += jnp.sum(e * e, axis=0, keepdims=True)
        sums_in[0, lc] = column

    @pl.loop(1, NROW)
    def _(d):
        for lc in range(CT):
            sums_out[d, lc] = sums_in[0, lc]
        sums_move(d).start()

    tiles_in[0], sums_in[0, CT] = coded(0)
    for make, *args in pending:
        make(*args).wait_send()

    @pl.loop(1, NROW)
    def _(d):
        sums_move(d).wait()
        tile_move(d).wait()

    for lc in range(CT):
        scale[lc] = float(NROW * RT * TS) / jnp.sum(sums_in[:, lc], axis=0)

    for u in range(UNITS):
        come = sroute[1, 0, u]
        d = jnp.clip((r + NROW - (come >> 3)) % NROW, 0, NROW - 1)
        e = tiles_in[d].astype(I32).astype(F32) * (sums_in[d, CT] * (1.0 / LEVELS))
        out[0, u] = ((e * e) * scale[come & (CT - 1)]).astype(BF16)


def body(tile_values, tile_index, keep_rows, slot_place):
    dma = pltpu.SemaphoreType.DMA
    anywhere = pl.BlockSpec(memory_space=pl.ANY)
    scratch = [pltpu.VMEM((SLOTS + 1, TS, TS), BF16)] * (1 + 7 + 7 + 8)
    scratch += [pltpu.SMEM((1, SLOTS), I32), pltpu.SMEM((KEEP, 64), I32), pltpu.SMEM((KEEP, 64), I32)]
    scratch += [pltpu.VMEM((8, 1, TS), I32)] * 3 + [pltpu.SMEM((8, 1, TS), I32)] * 3
    scratch += [
        pltpu.VMEM((2, 1, TS), I32),
        pltpu.SMEM((2, 1, TS), I32),
        pltpu.VMEM((NQ, RT * TS, CT * TS), BF16),
        pltpu.VMEM((NQ, NW, 2 * RT * TS, WIDE), BF16),
        pltpu.VMEM((RT * CT, TS, TS), F32),
        pltpu.VMEM((NROW, CT + 1, 1, TS), F32),
        pltpu.VMEM((NROW, CT + 1, 1, TS), F32),
        pltpu.VMEM((CT, 1, TS), F32),
        pltpu.VMEM((NROW, TS, TS), jnp.int16),
        pltpu.VMEM((NROW, TS, TS), jnp.int16),
    ]
    scratch += [dma((8, MOST))] * 6 + [dma((8,))] * 9 + [dma((NROW,))] * 4 + [dma((5,))]
    return pl.pallas_call(
        kernel,
        out_shape=jax.ShapeDtypeStruct((1, UNITS, TS, TS), BF16),
        in_specs=[anywhere] * 4,
        out_specs=pl.BlockSpec(memory_space=pltpu.VMEM),
        scratch_shapes=scratch,
        compiler_params=pltpu.CompilerParams(collective_id=0, has_side_effects=True, vmem_limit_bytes=56 * 2**20),
        cost_estimate=pl.CostEstimate(flops=2 * 512 * 8192 * 1024, bytes_accessed=2**20, transcendentals=0),
        name="clustering_step",
    )(tile_values, tile_index, keep_rows.T, slot_place.T)


def solution(mesh):
    placed = (P("row", "col", None, None), P("row", "col"), P(), P())
    return jax.shard_map(
        body, mesh=mesh, in_specs=placed, out_specs=P("col", "row", None, None), check_vma=False
    )
```

```python
import jax
import jax.numpy as jnp
from jax import lax
from jax.experimental import pallas as pl
from jax.experimental.pallas import tpu as pltpu
from jax.sharding import PartitionSpec as P

MESH = pl.DeviceIdType.MESH
TS = 128
RT = 4
CT = 8
SLOTS = 16
NROW = 16
NCOL = 8
KEEP = 8
UNITS = 4
NQ = 8
WIDE = 256
NW = CT * TS // WIDE
BATCH = 4
LEVELS = 32767.0
F32 = jnp.float32
I32 = jnp.int32
BF16 = jnp.bfloat16

BEHIND, AHEAD, PARTNER, FAR, BEHIND2, AHEAD2, FAR2, OWN = range(8)
NEAR_PIECES = {
    "+": [(0, 4, "+"), (4, 4, "+"), (8, 4, "+"), (12, 4, "+")],
    "-": [(8, 4, "-"), (12, 4, "-"), (0, 4, "-"), (4, 4, "-")],
    "z": [(0, 4, "z"), (12, 4, "z"), (4, 4, "z"), (8, 4, "z")],
}
FAR_PIECES = [(0, 4, "+"), (4, 4, "+"), (8, 4, "-"), (12, 4, "-")]
FAR2_PIECES = {
    "a": [(0, 4, "+"), (4, 2, "+"), (6, 2, "z"), (8, 2, "z"), (10, 2, "-"), (12, 4, "-")],
    "b": [(0, 4, "+"), (4, 4, "z"), (8, 4, "z"), (12, 4, "-")],
}
PIECES = {
    axis: {
        BEHIND: NEAR_PIECES["+"], AHEAD: NEAR_PIECES["-"], PARTNER: NEAR_PIECES["z"], FAR: FAR_PIECES,
        BEHIND2: [(s, n, "+") for s, n, _ in NEAR_PIECES["z"]], AHEAD2: [(s, n, "-") for s, n, _ in NEAR_PIECES["z"]],
        FAR2: FAR2_PIECES[axis], OWN: [(0, 4, ""), (4, 4, ""), (8, 4, ""), (12, 4, "")],
    }
    for axis in "ab"
}
MOST = 6
PARTNERS = (("a", 0), ("a", 1), ("b", 0), ("a", 2), ("a", 3), ("b", 1), ("b", 2), ("b", 3))
HELD = {"a": {(FAR, 0), (FAR, 1), (FAR, 2), (FAR, 3), (FAR2, 0), (FAR2, 1), (FAR2, 4), (FAR2, 5)}, "b": set()}
STEP = {
    "a": {OWN: 0, BEHIND: 1, AHEAD: 1, PARTNER: 2, BEHIND2: 3, AHEAD2: 3, FAR: 4, FAR2: 6},
    "b": {OWN: 0, BEHIND: 1, AHEAD: 1, FAR: 2, PARTNER: 3, BEHIND2: 5, AHEAD2: 5, FAR2: 7},
}
SLICES = {0: 1, 4: 1, 5: 1, 6: 1, 7: 1, 8: 1, 9: 2, 10: 2, 11: 2}


def origin(unit, way):
    if unit in (BEHIND, AHEAD, PARTNER):
        return OWN
    if unit in (BEHIND2, AHEAD2):
        return PARTNER
    if unit == FAR:
        return BEHIND if way == "+" else AHEAD
    return {"+": BEHIND2, "-": AHEAD2, "z": FAR}[way]


def follow_ups(axis, unit, i):
    first, count, _ = PIECES[axis][unit][i]
    found = []
    for nxt in (FAR, BEHIND2, AHEAD2, FAR2):
        for k, (s, n, way) in enumerate(PIECES[axis][nxt]):
            if origin(nxt, way) == unit and first <= s and s + n <= first + count:
                found.append((nxt, k))
    return found


def arrivals():
    free, waiting, done = {}, {}, []
    for axis in "ba":
        for unit in (PARTNER, BEHIND, AHEAD):
            for i, (_, n, way) in enumerate(PIECES[axis][unit]):
                first = PARTNERS.index((axis, i)) if unit == PARTNER else i
                link = way if way == "z" else axis + way
                waiting.setdefault(link, []).append((0.0, first, axis, unit, i, n / 4))
                free[link] = 0.0
    count, held, partner = 100, {"a": [], "b": []}, {"a": 4, "b": 4}
    while any(waiting.values()):
        link = min((n for n in waiting if waiting[n]), key=lambda n: (max(free[n], min(waiting[n])[0]), n))
        item = min(waiting[link], key=lambda m: (max(m[0], free[link]), m[1], m[2]))
        waiting[link].remove(item)
        ready, _, axis, unit, i, cost = item
        free[link] = max(free[link], ready) + cost
        partner[axis] -= unit == PARTNER
        sends = follow_ups(axis, unit, i)
        if partner[axis]:
            held[axis] += [m for m in sends if m in HELD[axis]]
            sends = [m for m in sends if m not in HELD[axis]]
        elif held[axis]:
            sends += sorted(held[axis])
            held[axis] = []
        done.append((free[link], axis, unit, i, sends))
        for nxt, k in sends:
            count += 1
            _, n, way = PIECES[axis][nxt][k]
            waiting[way if way == "z" else axis + way].append((free[link], count, axis, nxt, k, n / 4))
    return sorted(done, key=lambda m: m[0])


def eye_tile():
    rows = lax.broadcasted_iota(I32, (TS, TS), 0)
    cols = lax.broadcasted_iota(I32, (TS, TS), 1)
    return jnp.where(rows == cols, 1.0, 0.0).astype(F32)


def kernel(values, index_in, keep_in, place_in, out, own, *scratch):
    got_a, scratch = scratch[:7], scratch[7:]
    got_b, scratch = scratch[:7], scratch[7:]
    got_s, scratch = scratch[:8], scratch[8:]
    (
        index, keep, place,
        map_a, map_b, map_s, smap_a, smap_b, smap_s, route, sroute,
        dense_a, dense_b, total, sums_out, sums_in, scale, tiles_out, tiles_in,
        send_a, recv_a, send_b, recv_b, send_s, recv_s,
        msend_a, mrecv_a, msend_b, mrecv_b, msend_s, mrecv_s, mlocal_a, mlocal_b, mlocal_s,
        ssend, srecv, tsend, trecv, local,
    ) = scratch

    r = lax.axis_index("row")
    c = lax.axis_index("col")
    core = r % 2
    ring_pos = {"a": c // 2, "b": (r // 2) % 4}
    plane = {"a": c % 2, "b": r // 8}
    got = {"a": got_a, "b": got_b}
    send = {"a": send_a, "b": send_b}
    recv = {"a": recv_a, "b": recv_b}
    maps = {"a": map_a, "b": map_b, "s": map_s}
    smaps = {"a": smap_a, "b": smap_b, "s": smap_s}
    msend = {"a": msend_a, "b": msend_b}
    mrecv = {"a": mrecv_a, "b": mrecv_b}
    mlocal = {"a": mlocal_a, "b": mlocal_b, "s": mlocal_s}
    pending = []

    def block_of(axis, pos, side):
        return pos * 2 + side if axis == "a" else side * 8 + pos * 2 + core

    def device_of(axis, pos, side):
        block = block_of(axis, pos, side)
        return (r, block) if axis == "a" else (block, c)

    def towards(axis, way):
        pos, side = ring_pos[axis], plane[axis]
        if way == "z":
            return device_of(axis, pos, 1 - side)
        return device_of(axis, (pos + (1 if way == "+" else 3)) % 4, side)

    sibling = (r + 1 - 2 * core, c)

    index_copy = pltpu.make_async_copy(index_in, index, local.at[2])
    index_copy.start()
    own_copy = pltpu.make_async_copy(values.at[0], own.at[pl.ds(0, SLOTS)], local.at[0])
    own_copy.start()

    barrier = pltpu.get_barrier_semaphore()
    neighbours = [sibling] + [towards(axis, way) for axis in "ab" for way in "+-z"]
    for device in neighbours:
        pl.semaphore_signal(barrier, inc=1, device_id=device, device_id_type=MESH)
    pl.semaphore_wait(barrier, len(neighbours))

    def remote(src, dst, send_sem, recv_sem, device):
        return pltpu.make_async_remote_copy(
            src_ref=src, dst_ref=dst, send_sem=send_sem, recv_sem=recv_sem, device_id=device, device_id_type=MESH
        )

    def part(ref, piece):
        return ref.at[pl.ds(piece[0], piece[1])]

    def bulk(axis, unit, i):
        piece = PIECES[axis][unit][i]
        source = origin(unit, piece[2])
        src = values.at[0] if source == OWN else got[axis][source]
        return remote(
            part(src, piece), part(got[axis][unit], piece), send[axis].at[unit, i], recv[axis].at[unit, i], towards(axis, piece[2])
        )

    def across(unit, i):
        piece = PIECES["b"][unit][i]
        src = values.at[0] if unit == OWN else got_b[unit]
        return remote(part(src, piece), part(got_s[unit], piece), send_s.at[unit, i], recv_s.at[unit, i], sibling)

    def map_copy(axis, unit):
        way = "z" if unit == PARTNER else "-" if unit in (AHEAD, AHEAD2) else "+"
        ref = maps[axis]
        return remote(ref.at[origin(unit, way)], ref.at[unit], msend[axis].at[unit], mrecv[axis].at[unit], towards(axis, way))

    def map_across(unit):
        return remote(map_b.at[unit], map_s.at[unit], msend_s.at[unit], mrecv_s.at[unit], sibling)

    def map_inward(axis, unit):
        return pltpu.make_async_copy(maps[axis].at[unit], smaps[axis].at[unit], mlocal[axis].at[unit])

    def start_all(*copies):
        for make, *args in copies:
            make(*args).start()
            pending.append((make, *args))

    def pass_map(axis, unit):
        map_copy(axis, unit).wait_recv()
        onward = {BEHIND: [FAR], PARTNER: [BEHIND2, AHEAD2], BEHIND2: [FAR2]}.get(unit, [])
        start_all(*[(map_copy, axis, nxt) for nxt in onward])
        map_inward(axis, unit).start()
        if axis == "b":
            start_all((map_across, unit))

    def start_own(i):
        for axis, k in PARTNERS[2 * i : 2 * i + 2]:
            start_all((bulk, axis, PARTNER, k))
        for axis in "ba":
            start_all((bulk, axis, BEHIND, i), (bulk, axis, AHEAD, i))

    start_own(0)
    index_copy.wait()
    lane = lax.broadcasted_iota(I32, (1, TS), 1)
    slot_of = jnp.full((1, TS), SLOTS, I32)
    for s in range(SLOTS):
        slot_of = jnp.where(lane == index[0, s], s, slot_of)
    map_a[OWN] = slot_of
    map_b[OWN] = slot_of
    for axis in "ab":
        start_all(*[(map_copy, axis, unit) for unit in (BEHIND, AHEAD, PARTNER)])
        map_inward(axis, OWN).start()
    start_all((map_across, OWN))
    for i in range(1, 4):
        start_own(i)
    for i in range(4):
        start_all((across, OWN, i))
    list_copies = [pltpu.make_async_copy(keep_in, keep, local.at[3]), pltpu.make_async_copy(place_in, place, local.at[4])]
    for copy in list_copies:
        copy.start()

    total[...] = jnp.zeros_like(total)
    for block in (own, *got_a, *got_b, *got_s):
        block[SLOTS] = jnp.zeros((TS, TS), BF16)
    for copy in list_copies:
        copy.wait()

    def entry(e, carry):
        sending, coming = carry
        kept = keep[e % KEEP, c * CT + e // KEEP]
        slot = place[e % KEEP, c * CT + e // KEEP]
        holder, owner = kept >> 2, slot >> 2
        sending = jnp.where((lane == owner) & (holder == r), (kept & 3) * CT + e // KEEP, sending)
        coming = jnp.where((lane == (slot & 3)) & (owner == r), holder * CT + e // KEEP, coming)
        return sending, coming

    nothing = jnp.zeros((1, TS), I32)
    sending, coming = lax.fori_loop(0, CT * KEEP, entry, (nothing, nothing))
    route[0] = sending
    route[1] = coming
    route_copy = pltpu.make_async_copy(route, sroute, local.at[1])
    route_copy.start()
    own_copy.wait()

    def lay_rows(block, smap, unit, store):
        @pl.loop(0, RT)
        def _(lr):
            for first in range(0, CT, BATCH):
                some = range(first, first + BATCH)
                tiles = [block[smap[unit, 0, lr * CT + lc]] for lc in some]
                for lc, tile in zip(some, tiles):
                    store(lr, lc, tile)

    def lay_a(block, smap, unit, q):
        def store(lr, lc, tile):
            rows = pl.ds(pl.multiple_of(lr * TS, TS), TS)
            dense_a[q, rows, lc * TS : (lc + 1) * TS] = tile

        lay_rows(block, smap, unit, store)

    def lay_b(block, smap, unit, p):
        q, upper = p // 2, p % 2

        def store(lr, lc, tile):
            rows = pl.ds(pl.multiple_of((upper * RT + lr) * TS, TS), TS)
            j = lc % 2
            dense_b[q, lc // 2, rows, j * TS : (j + 1) * TS] = tile

        lay_rows(block, smap, unit, store)

    def position(axis, unit):
        pos, side = ring_pos[axis], plane[axis]
        shift = {OWN: 0, BEHIND: 3, AHEAD: 1, PARTNER: 0, FAR: 2, BEHIND2: 3, AHEAD2: 1, FAR2: 2}[unit]
        other = unit in (PARTNER, BEHIND2, AHEAD2, FAR2)
        return block_of(axis, (pos + shift) % 4, 1 - side if other else side)

    def lay(which, unit):
        if which == "s":
            for i in range(len(PIECES["b"][unit])):
                across(unit, i).wait_recv()
            map_across(unit).wait_recv()
            inward = map_inward("s", unit)
            inward.start()
            inward.wait()
            lay_b(got_s[unit], smap_s, unit, position("b", unit) + 1 - 2 * core)
            return
        block = own if unit == OWN else got[which][unit]
        map_inward(which, unit).wait()
        (lay_a if which == "a" else lay_b)(block, smaps[which], unit, position(which, unit))

    def step_of(axis, pos, side):
        steps = STEP[axis]
        shift = (pos + 4 - ring_pos[axis]) % 4
        same = side == plane[axis]
        first = jnp.where(same, steps[OWN], steps[PARTNER])
        near = jnp.where(same, steps[BEHIND], steps[BEHIND2])
        far = jnp.where(same, steps[FAR], steps[FAR2])
        return jnp.where(shift == 0, first, jnp.where(shift == 2, far, near))

    def add_eyes(q):
        @pl.when(q == r // 2)
        def _():
            for lr in range(RT):
                cols = pl.ds(pl.multiple_of((core * RT + lr) * TS, TS), TS)
                rows = slice(lr * TS, (lr + 1) * TS)
                dense_a[q, rows, cols] = (dense_a[q, rows, cols].astype(F32) + eye_tile()).astype(BF16)

        @pl.when(q == c)
        def _():
            for lc in range(CT):
                j = lc % 2
                at = (q, lc // 2, slice(lc * TS, (lc + 1) * TS), slice(j * TS, (j + 1) * TS))
                dense_b[at] = (dense_b[at].astype(F32) + eye_tile()).astype(BF16)

    def multiply(q):
        add_eyes(q)
        for n in range(NW):
            product = jnp.dot(dense_a[q], dense_b[q, n], preferred_element_type=F32)
            for lr in range(RT):
                for j in range(WIDE // TS):
                    tile = product[lr * TS : (lr + 1) * TS, j * TS : (j + 1) * TS]
                    total[lr * CT + n * (WIDE // TS) + j] += tile

    events = arrivals()
    missing = {(axis, unit): len(PIECES[axis][unit]) for axis in "ab" for unit in range(OWN)}
    for axis in "ab":
        missing[axis, OWN] = 0
    left = [(axis, unit) for step in range(8) for axis in "ab" for unit in STEP[axis] if STEP[axis][unit] == step]
    phases = []
    for when in sorted({0.0} | {event[0] for event in events}):
        now = [event for event in events if event[0] == when]
        for _, axis, unit, _, _ in now:
            missing[axis, unit] -= 1
        lays = []
        while left and not missing[left[0]] and left[0] != ("b", FAR2):
            lays.append(left.pop(0))
        step = max(-1, min([STEP[axis][unit] for axis, unit in left]) - 1)
        if when % 1 and when < 11:
            carried = now
            phases.append([carried, lays, step, 0])
        else:
            phases.append([now, lays, step, SLICES.get(when, 8 if when > 11 else 0)])
    phases.append([[], left, 7, 8])
    merged = []
    for phase in phases:
        if merged and merged[-1][3] == 0:
            before = merged.pop()
            phase = [before[0] + phase[0], before[1] + phase[1], phase[2], phase[3]]
        merged.append(phase)
    phases = merged
    counts = {(axis, unit): len(PIECES[axis][unit]) for axis in "ab" for unit in range(OWN)}

    needs = [jnp.maximum(step_of("a", q // 2, q % 2), step_of("b", q % 4, q // 4)) for q in range(NQ)]
    places = []

    def total_of(terms):
        return sum(terms[1:], terms[0])

    for q in range(NQ):
        before = [(needs[p] <= needs[q] if p < q else needs[p] < needs[q]).astype(I32) for p in range(NQ) if p != q]
        places.append(total_of(before))

    def phase_work(phase):
        for _, axis, unit, k, sends in phase[0]:
            bulk(axis, unit, k).wait_recv()
            start_all(*[(bulk, axis, nxt, kk) for nxt, kk in sends])
            if axis == "b":
                start_all((across, unit, k))
            counts[axis, unit] -= 1
            if counts[axis, unit] == (2 if unit in (BEHIND, PARTNER, BEHIND2) else 0):
                pass_map(axis, unit)
        for axis, unit in phase[1]:
            lay(axis, unit)
            if axis == "b":
                lay("s", unit)

    def one_phase(t, done):
        for i, phase in enumerate(phases):
            pl.when(t == i)(lambda phase=phase: phase_work(phase))
        upto = total_of([(t == i).astype(I32) * phase[2] for i, phase in enumerate(phases)])
        most = total_of([(t == i).astype(I32) * phase[3] for i, phase in enumerate(phases)])
        ready = total_of([(n <= upto).astype(I32) for n in needs])
        until = jnp.maximum(done, jnp.minimum(done + most, ready))

        def one_slice(j, carry):
            q = total_of([(p == j).astype(I32) * i for i, p in enumerate(places)])
            multiply(q)
            return carry

        lax.fori_loop(done, until, one_slice, 0)
        return until

    lax.fori_loop(0, len(phases), one_phase, r * 0)

    route_copy.wait()

    def coded(d):
        e = total[jnp.clip(sroute[0, 0, (r + d) % NROW], 0, RT * CT - 1)]
        top = jnp.max(jnp.abs(e), axis=0, keepdims=True)
        steps_per = jnp.where(top > 0, LEVELS / top, 0.0)
        return jnp.floor(e * steps_per + 0.5).astype(I32).astype(jnp.int16), top

    def tile_move(d):
        return remote(tiles_out.at[d], tiles_in.at[d], tsend.at[d], trecv.at[d], ((r + d) % NROW, c))

    def sums_move(d):
        return remote(sums_out.at[d], sums_in.at[d], ssend.at[d], srecv.at[d], ((r + d) % NROW, c))

    @pl.loop(0, NROW - 1)
    def _(i):
        d = NROW // 2 + (i % 2) * ((i + 1) // 2) - (1 - i % 2) * (i // 2)
        tiles_out[d], sums_out[d, CT] = coded(d)
        tile_move(d).start()

    for lc in range(CT):
        column = jnp.zeros((1, TS), F32)
        for lr in range(RT):
            e = total[lr * CT + lc]
            column += jnp.sum(e * e, axis=0, keepdims=True)
        sums_in[0, lc] = column

    @pl.loop(1, NROW)
    def _(d):
        for lc in range(CT):
            sums_out[d, lc] = sums_in[0, lc]
        sums_move(d).start()

    tiles_in[0], sums_in[0, CT] = coded(0)
    for make, *args in pending:
        make(*args).wait_send()

    @pl.loop(1, NROW)
    def _(d):
        sums_move(d).wait()
        tile_move(d).wait()

    for lc in range(CT):
        scale[lc] = float(NROW * RT * TS) / jnp.sum(sums_in[:, lc], axis=0)

    for u in range(UNITS):
        come = sroute[1, 0, u]
        d = jnp.clip((r + NROW - (come >> 3)) % NROW, 0, NROW - 1)
        e = tiles_in[d].astype(I32).astype(F32) * (sums_in[d, CT] * (1.0 / LEVELS))
        out[0, u] = ((e * e) * scale[come & (CT - 1)]).astype(BF16)


def body(tile_values, tile_index, keep_rows, slot_place):
    dma = pltpu.SemaphoreType.DMA
    anywhere = pl.BlockSpec(memory_space=pl.ANY)
    scratch = [pltpu.VMEM((SLOTS + 1, TS, TS), BF16)] * (1 + 7 + 7 + 8)
    scratch += [pltpu.SMEM((1, SLOTS), I32), pltpu.SMEM((KEEP, 64), I32), pltpu.SMEM((KEEP, 64), I32)]
    scratch += [pltpu.VMEM((8, 1, TS), I32)] * 3 + [pltpu.SMEM((8, 1, TS), I32)] * 3
    scratch += [
        pltpu.VMEM((2, 1, TS), I32),
        pltpu.SMEM((2, 1, TS), I32),
        pltpu.VMEM((NQ, RT * TS, CT * TS), BF16),
        pltpu.VMEM((NQ, NW, 2 * RT * TS, WIDE), BF16),
        pltpu.VMEM((RT * CT, TS, TS), F32),
        pltpu.VMEM((NROW, CT + 1, 1, TS), F32),
        pltpu.VMEM((NROW, CT + 1, 1, TS), F32),
        pltpu.VMEM((CT, 1, TS), F32),
        pltpu.VMEM((NROW, TS, TS), jnp.int16),
        pltpu.VMEM((NROW, TS, TS), jnp.int16),
    ]
    scratch += [dma((8, MOST))] * 6 + [dma((8,))] * 9 + [dma((NROW,))] * 4 + [dma((5,))]
    return pl.pallas_call(
        kernel,
        out_shape=jax.ShapeDtypeStruct((1, UNITS, TS, TS), BF16),
        in_specs=[anywhere] * 4,
        out_specs=pl.BlockSpec(memory_space=pltpu.VMEM),
        scratch_shapes=scratch,
        compiler_params=pltpu.CompilerParams(collective_id=0, has_side_effects=True, vmem_limit_bytes=56 * 2**20),
        cost_estimate=pl.CostEstimate(flops=2 * 512 * 8192 * 1024, bytes_accessed=2**20, transcendentals=0),
        name="clustering_step",
    )(tile_values, tile_index, keep_rows.T, slot_place.T)


def solution(mesh):
    placed = (P("row", "col", None, None), P("row", "col"), P(), P())
    return jax.shard_map(
        body, mesh=mesh, in_specs=placed, out_specs=P("col", "row", None, None), check_vma=False
    )
```

```python
import jax
import jax.numpy as jnp
from jax import lax
from jax.experimental import pallas as pl
from jax.experimental.pallas import tpu as pltpu
from jax.sharding import PartitionSpec as P

MESH = pl.DeviceIdType.MESH
TS = 128
RT = 4
CT = 8
SLOTS = 16
NROW = 16
NCOL = 8
KEEP = 8
UNITS = 4
NQ = 8
WIDE = 256
NW = CT * TS // WIDE
BATCH = 4
LEVELS = 32767.0
F32 = jnp.float32
I32 = jnp.int32
BF16 = jnp.bfloat16

BEHIND, AHEAD, PARTNER, FAR, BEHIND2, AHEAD2, FAR2, OWN = range(8)
NEAR_PIECES = {
    "+": [(0, 4, "+"), (4, 4, "+"), (8, 4, "+"), (12, 4, "+")],
    "-": [(8, 4, "-"), (12, 4, "-"), (0, 4, "-"), (4, 4, "-")],
    "z": [(0, 4, "z"), (12, 4, "z"), (4, 4, "z"), (8, 4, "z")],
}
FAR_PIECES = [(0, 4, "+"), (4, 4, "+"), (8, 4, "-"), (12, 4, "-")]
FAR2_PIECES = {
    "a": [(0, 4, "+"), (4, 2, "+"), (6, 2, "z"), (8, 2, "z"), (10, 2, "-"), (12, 4, "-")],
    "b": [(0, 4, "+"), (4, 4, "z"), (8, 4, "z"), (12, 4, "-")],
}
PIECES = {
    axis: {
        BEHIND: NEAR_PIECES["+"], AHEAD: NEAR_PIECES["-"], PARTNER: NEAR_PIECES["z"], FAR: FAR_PIECES,
        BEHIND2: [(s, n, "+") for s, n, _ in NEAR_PIECES["z"]], AHEAD2: [(s, n, "-") for s, n, _ in NEAR_PIECES["z"]],
        FAR2: FAR2_PIECES[axis], OWN: [(0, 4, ""), (4, 4, ""), (8, 4, ""), (12, 4, "")],
    }
    for axis in "ab"
}
MOST = 6
PARTNERS = (("a", 0), ("a", 1), ("b", 0), ("a", 2), ("a", 3), ("b", 1), ("b", 2), ("b", 3))
HELD = {"a": {(FAR, 0), (FAR, 1), (FAR, 2), (FAR, 3), (FAR2, 0), (FAR2, 1), (FAR2, 4), (FAR2, 5)}, "b": {(FAR2, 0), (FAR2, 3)}}
STEP = {
    "a": {OWN: 0, BEHIND: 1, AHEAD: 1, PARTNER: 2, BEHIND2: 3, AHEAD2: 3, FAR: 4, FAR2: 6},
    "b": {OWN: 0, BEHIND: 1, AHEAD: 1, FAR: 2, PARTNER: 3, BEHIND2: 5, AHEAD2: 5, FAR2: 7},
}
SLICES = {0: 1, 4: 1, 6: 1, 8: 1, 9: 2, 10: 2, 11: 8}


def origin(unit, way):
    if unit in (BEHIND, AHEAD, PARTNER):
        return OWN
    if unit in (BEHIND2, AHEAD2):
        return PARTNER
    if unit == FAR:
        return BEHIND if way == "+" else AHEAD
    return {"+": BEHIND2, "-": AHEAD2, "z": FAR}[way]


def follow_ups(axis, unit, i):
    first, count, _ = PIECES[axis][unit][i]
    found = []
    for nxt in (FAR, BEHIND2, AHEAD2, FAR2):
        for k, (s, n, way) in enumerate(PIECES[axis][nxt]):
            if origin(nxt, way) == unit and first <= s and s + n <= first + count:
                found.append((nxt, k))
    return found


def arrivals():
    free, waiting, done = {}, {}, []
    for axis in "ba":
        for unit in (PARTNER, BEHIND, AHEAD):
            for i, (_, n, way) in enumerate(PIECES[axis][unit]):
                first = PARTNERS.index((axis, i)) if unit == PARTNER else i
                link = way if way == "z" else axis + way
                waiting.setdefault(link, []).append((0.0, first, axis, unit, i, n / 4))
                free[link] = 0.0
    count, held, partner = 100, {"a": [], "b": []}, {"a": 4, "b": 4}
    while any(waiting.values()):
        link = min((n for n in waiting if waiting[n]), key=lambda n: (max(free[n], min(waiting[n])[0]), n))
        item = min(waiting[link], key=lambda m: (max(m[0], free[link]), m[1], m[2]))
        waiting[link].remove(item)
        ready, _, axis, unit, i, cost = item
        free[link] = max(free[link], ready) + cost
        partner[axis] -= unit == PARTNER
        sends = follow_ups(axis, unit, i)
        if partner[axis]:
            held[axis] += [m for m in sends if m in HELD[axis]]
            sends = [m for m in sends if m not in HELD[axis]]
        elif held[axis]:
            sends += sorted(held[axis])
            held[axis] = []
        done.append((free[link], axis, unit, i, sends))
        for nxt, k in sends:
            count += 1
            _, n, way = PIECES[axis][nxt][k]
            waiting[way if way == "z" else axis + way].append((free[link], count, axis, nxt, k, n / 4))
    return sorted(done, key=lambda m: m[0])


def eye_tile():
    rows = lax.broadcasted_iota(I32, (TS, TS), 0)
    cols = lax.broadcasted_iota(I32, (TS, TS), 1)
    return jnp.where(rows == cols, 1.0, 0.0).astype(F32)


def kernel(values, index_in, keep_in, place_in, out, own, *scratch):
    got_a, scratch = scratch[:7], scratch[7:]
    got_b, scratch = scratch[:7], scratch[7:]
    got_s, scratch = scratch[:8], scratch[8:]
    (
        index, keep, place,
        map_a, map_b, map_s, smap_a, smap_b, smap_s, route, sroute,
        dense_a, dense_b, total, sums_out, sums_in, scale, tiles_out, tiles_in,
        send_a, recv_a, send_b, recv_b, send_s, recv_s,
        msend_a, mrecv_a, msend_b, mrecv_b, msend_s, mrecv_s, mlocal_a, mlocal_b, mlocal_s,
        ssend, srecv, tsend, trecv, local,
    ) = scratch

    r = lax.axis_index("row")
    c = lax.axis_index("col")
    core = r % 2
    ring_pos = {"a": c // 2, "b": (r // 2) % 4}
    plane = {"a": c % 2, "b": r // 8}
    got = {"a": got_a, "b": got_b}
    send = {"a": send_a, "b": send_b}
    recv = {"a": recv_a, "b": recv_b}
    maps = {"a": map_a, "b": map_b, "s": map_s}
    smaps = {"a": smap_a, "b": smap_b, "s": smap_s}
    msend = {"a": msend_a, "b": msend_b}
    mrecv = {"a": mrecv_a, "b": mrecv_b}
    mlocal = {"a": mlocal_a, "b": mlocal_b, "s": mlocal_s}
    pending = []

    def block_of(axis, pos, side):
        return pos * 2 + side if axis == "a" else side * 8 + pos * 2 + core

    def device_of(axis, pos, side):
        block = block_of(axis, pos, side)
        return (r, block) if axis == "a" else (block, c)

    def towards(axis, way):
        pos, side = ring_pos[axis], plane[axis]
        if way == "z":
            return device_of(axis, pos, 1 - side)
        return device_of(axis, (pos + (1 if way == "+" else 3)) % 4, side)

    sibling = (r + 1 - 2 * core, c)

    index_copy = pltpu.make_async_copy(index_in, index, local.at[2])
    index_copy.start()
    own_copy = pltpu.make_async_copy(values.at[0], own.at[pl.ds(0, SLOTS)], local.at[0])
    own_copy.start()

    barrier = pltpu.get_barrier_semaphore()
    neighbours = [sibling] + [towards(axis, way) for axis in "ab" for way in "+-z"]
    for device in neighbours:
        pl.semaphore_signal(barrier, inc=1, device_id=device, device_id_type=MESH)
    pl.semaphore_wait(barrier, len(neighbours))

    def remote(src, dst, send_sem, recv_sem, device):
        return pltpu.make_async_remote_copy(
            src_ref=src, dst_ref=dst, send_sem=send_sem, recv_sem=recv_sem, device_id=device, device_id_type=MESH
        )

    def part(ref, piece):
        return ref.at[pl.ds(piece[0], piece[1])]

    def bulk(axis, unit, i):
        piece = PIECES[axis][unit][i]
        source = origin(unit, piece[2])
        src = values.at[0] if source == OWN else got[axis][source]
        return remote(
            part(src, piece), part(got[axis][unit], piece), send[axis].at[unit, i], recv[axis].at[unit, i], towards(axis, piece[2])
        )

    def across(unit, i):
        piece = PIECES["b"][unit][i]
        src = values.at[0] if unit == OWN else got_b[unit]
        return remote(part(src, piece), part(got_s[unit], piece), send_s.at[unit, i], recv_s.at[unit, i], sibling)

    def map_copy(axis, unit):
        way = "z" if unit == PARTNER else "-" if unit in (AHEAD, AHEAD2) else "+"
        ref = maps[axis]
        return remote(ref.at[origin(unit, way)], ref.at[unit], msend[axis].at[unit], mrecv[axis].at[unit], towards(axis, way))

    def map_across(unit):
        return remote(map_b.at[unit], map_s.at[unit], msend_s.at[unit], mrecv_s.at[unit], sibling)

    def map_inward(axis, unit):
        return pltpu.make_async_copy(maps[axis].at[unit], smaps[axis].at[unit], mlocal[axis].at[unit])

    def start_all(*copies):
        for make, *args in copies:
            make(*args).start()
            pending.append((make, *args))

    def pass_map(axis, unit):
        map_copy(axis, unit).wait_recv()
        onward = {BEHIND: [FAR], PARTNER: [BEHIND2, AHEAD2], BEHIND2: [FAR2]}.get(unit, [])
        start_all(*[(map_copy, axis, nxt) for nxt in onward])
        map_inward(axis, unit).start()
        if axis == "b":
            start_all((map_across, unit))

    def start_own(i):
        for axis, k in PARTNERS[2 * i : 2 * i + 2]:
            start_all((bulk, axis, PARTNER, k))
        for axis in "ba":
            start_all((bulk, axis, BEHIND, i), (bulk, axis, AHEAD, i))

    start_own(0)
    index_copy.wait()
    lane = lax.broadcasted_iota(I32, (1, TS), 1)
    slot_of = jnp.full((1, TS), SLOTS, I32)
    for s in range(SLOTS):
        slot_of = jnp.where(lane == index[0, s], s, slot_of)
    map_a[OWN] = slot_of
    map_b[OWN] = slot_of
    for axis in "ab":
        start_all(*[(map_copy, axis, unit) for unit in (BEHIND, AHEAD, PARTNER)])
        map_inward(axis, OWN).start()
    start_all((map_across, OWN))
    for i in range(1, 4):
        start_own(i)
    for i in range(4):
        start_all((across, OWN, i))
    list_copies = [pltpu.make_async_copy(keep_in, keep, local.at[3]), pltpu.make_async_copy(place_in, place, local.at[4])]
    for copy in list_copies:
        copy.start()

    total[...] = jnp.zeros_like(total)
    for block in (own, *got_a, *got_b, *got_s):
        block[SLOTS] = jnp.zeros((TS, TS), BF16)
    for copy in list_copies:
        copy.wait()

    def entry(e, carry):
        sending, coming = carry
        kept = keep[e % KEEP, c * CT + e // KEEP]
        slot = place[e % KEEP, c * CT + e // KEEP]
        holder, owner = kept >> 2, slot >> 2
        sending = jnp.where((lane == owner) & (holder == r), (kept & 3) * CT + e // KEEP, sending)
        coming = jnp.where((lane == (slot & 3)) & (owner == r), holder * CT + e // KEEP, coming)
        return sending, coming

    nothing = jnp.zeros((1, TS), I32)
    sending, coming = lax.fori_loop(0, CT * KEEP, entry, (nothing, nothing))
    route[0] = sending
    route[1] = coming
    route_copy = pltpu.make_async_copy(route, sroute, local.at[1])
    route_copy.start()
    own_copy.wait()

    def lay_rows(block, smap, unit, store):
        @pl.loop(0, RT)
        def _(lr):
            for first in range(0, CT, BATCH):
                some = range(first, first + BATCH)
                tiles = [block[smap[unit, 0, lr * CT + lc]] for lc in some]
                for lc, tile in zip(some, tiles):
                    store(lr, lc, tile)

    def lay_a(block, smap, unit, q):
        def store(lr, lc, tile):
            rows = pl.ds(pl.multiple_of(lr * TS, TS), TS)
            dense_a[q, rows, lc * TS : (lc + 1) * TS] = tile

        lay_rows(block, smap, unit, store)

    def lay_b(block, smap, unit, p):
        q, upper = p // 2, p % 2

        def store(lr, lc, tile):
            rows = pl.ds(pl.multiple_of((upper * RT + lr) * TS, TS), TS)
            j = lc % 2
            dense_b[q, lc // 2, rows, j * TS : (j + 1) * TS] = tile

        lay_rows(block, smap, unit, store)

    def position(axis, unit):
        pos, side = ring_pos[axis], plane[axis]
        shift = {OWN: 0, BEHIND: 3, AHEAD: 1, PARTNER: 0, FAR: 2, BEHIND2: 3, AHEAD2: 1, FAR2: 2}[unit]
        other = unit in (PARTNER, BEHIND2, AHEAD2, FAR2)
        return block_of(axis, (pos + shift) % 4, 1 - side if other else side)

    def lay(which, unit):
        if which == "s":
            for i in range(len(PIECES["b"][unit])):
                across(unit, i).wait_recv()
            map_across(unit).wait_recv()
            inward = map_inward("s", unit)
            inward.start()
            inward.wait()
            lay_b(got_s[unit], smap_s, unit, position("b", unit) + 1 - 2 * core)
            return
        block = own if unit == OWN else got[which][unit]
        map_inward(which, unit).wait()
        (lay_a if which == "a" else lay_b)(block, smaps[which], unit, position(which, unit))

    def step_of(axis, pos, side):
        steps = STEP[axis]
        shift = (pos + 4 - ring_pos[axis]) % 4
        same = side == plane[axis]
        first = jnp.where(same, steps[OWN], steps[PARTNER])
        near = jnp.where(same, steps[BEHIND], steps[BEHIND2])
        far = jnp.where(same, steps[FAR], steps[FAR2])
        return jnp.where(shift == 0, first, jnp.where(shift == 2, far, near))

    def add_eyes(q):
        @pl.when(q == r // 2)
        def _():
            for lr in range(RT):
                cols = pl.ds(pl.multiple_of((core * RT + lr) * TS, TS), TS)
                rows = slice(lr * TS, (lr + 1) * TS)
                dense_a[q, rows, cols] = (dense_a[q, rows, cols].astype(F32) + eye_tile()).astype(BF16)

        @pl.when(q == c)
        def _():
            for lc in range(CT):
                j = lc % 2
                at = (q, lc // 2, slice(lc * TS, (lc + 1) * TS), slice(j * TS, (j + 1) * TS))
                dense_b[at] = (dense_b[at].astype(F32) + eye_tile()).astype(BF16)

    def multiply(q):
        add_eyes(q)
        for n in range(NW):
            product = jnp.dot(dense_a[q], dense_b[q, n], preferred_element_type=F32)
            for lr in range(RT):
                for j in range(WIDE // TS):
                    tile = product[lr * TS : (lr + 1) * TS, j * TS : (j + 1) * TS]
                    total[lr * CT + n * (WIDE // TS) + j] += tile

    events = arrivals()
    missing = {(axis, unit): len(PIECES[axis][unit]) for axis in "ab" for unit in range(OWN)}
    for axis in "ab":
        missing[axis, OWN] = 0
    left = [(axis, unit) for step in range(8) for axis in "ab" for unit in STEP[axis] if STEP[axis][unit] == step]
    phases = []
    for when in sorted({0.0} | {event[0] for event in events}):
        now = [event for event in events if event[0] == when]
        for _, axis, unit, _, _ in now:
            missing[axis, unit] -= 1
        lays = []
        while left and not missing[left[0]] and left[0] != ("b", FAR2):
            lays.append(left.pop(0))
        step = max(-1, min([STEP[axis][unit] for axis, unit in left]) - 1)
        if when % 1 and when < 11:
            carried = now
            phases.append([carried, lays, step, 0])
        else:
            phases.append([now, lays, step, SLICES.get(when, 8 if when > 11 else 0)])
    phases.append([[], left, 7, 8])
    merged = []
    for phase in phases:
        if merged and merged[-1][3] == 0:
            before = merged.pop()
            phase = [before[0] + phase[0], before[1] + phase[1], phase[2], phase[3]]
        merged.append(phase)
    phases = merged
    counts = {(axis, unit): len(PIECES[axis][unit]) for axis in "ab" for unit in range(OWN)}

    needs = [jnp.maximum(step_of("a", q // 2, q % 2), step_of("b", q % 4, q // 4)) for q in range(NQ)]
    places = []

    def total_of(terms):
        return sum(terms[1:], terms[0])

    for q in range(NQ):
        before = [(needs[p] <= needs[q] if p < q else needs[p] < needs[q]).astype(I32) for p in range(NQ) if p != q]
        places.append(total_of(before))

    def phase_work(phase):
        for _, axis, unit, k, sends in phase[0]:
            bulk(axis, unit, k).wait_recv()
            start_all(*[(bulk, axis, nxt, kk) for nxt, kk in sends])
            if axis == "b":
                start_all((across, unit, k))
            counts[axis, unit] -= 1
            if counts[axis, unit] == (2 if unit in (BEHIND, PARTNER, BEHIND2) else 0):
                pass_map(axis, unit)
        for axis, unit in phase[1]:
            lay(axis, unit)
            if axis == "b":
                lay("s", unit)

    def one_phase(t, done):
        for i, phase in enumerate(phases):
            pl.when(t == i)(lambda phase=phase: phase_work(phase))
        upto = total_of([(t == i).astype(I32) * phase[2] for i, phase in enumerate(phases)])
        most = total_of([(t == i).astype(I32) * phase[3] for i, phase in enumerate(phases)])
        ready = total_of([(n <= upto).astype(I32) for n in needs])
        until = jnp.maximum(done, jnp.minimum(done + most, ready))

        def one_slice(j, carry):
            q = total_of([(p == j).astype(I32) * i for i, p in enumerate(places)])
            multiply(q)
            return carry

        lax.fori_loop(done, until, one_slice, 0)
        return until

    lax.fori_loop(0, len(phases), one_phase, r * 0)

    route_copy.wait()

    def coded(d):
        e = total[jnp.clip(sroute[0, 0, (r + d) % NROW], 0, RT * CT - 1)]
        top = jnp.max(jnp.abs(e), axis=0, keepdims=True)
        steps_per = jnp.where(top > 0, LEVELS / top, 0.0)
        return jnp.floor(e * steps_per + 0.5).astype(I32).astype(jnp.int16), top

    def tile_move(d):
        return remote(tiles_out.at[d], tiles_in.at[d], tsend.at[d], trecv.at[d], ((r + d) % NROW, c))

    def sums_move(d):
        return remote(sums_out.at[d], sums_in.at[d], ssend.at[d], srecv.at[d], ((r + d) % NROW, c))

    @pl.loop(0, NROW - 1)
    def _(i):
        d = NROW // 2 + (i % 2) * ((i + 1) // 2) - (1 - i % 2) * (i // 2)
        tiles_out[d], sums_out[d, CT] = coded(d)
        tile_move(d).start()

    for lc in range(CT):
        column = jnp.zeros((1, TS), F32)
        for lr in range(RT):
            e = total[lr * CT + lc]
            column += jnp.sum(e * e, axis=0, keepdims=True)
        sums_in[0, lc] = column

    @pl.loop(1, NROW)
    def _(d):
        for lc in range(CT):
            sums_out[d, lc] = sums_in[0, lc]
        sums_move(d).start()

    tiles_in[0], sums_in[0, CT] = coded(0)
    for make, *args in pending:
        make(*args).wait_send()

    @pl.loop(1, NROW)
    def _(d):
        sums_move(d).wait()
        tile_move(d).wait()

    for lc in range(CT):
        scale[lc] = float(NROW * RT * TS) / jnp.sum(sums_in[:, lc], axis=0)

    for u in range(UNITS):
        come = sroute[1, 0, u]
        d = jnp.clip((r + NROW - (come >> 3)) % NROW, 0, NROW - 1)
        e = tiles_in[d].astype(I32).astype(F32) * (sums_in[d, CT] * (1.0 / LEVELS))
        out[0, u] = ((e * e) * scale[come & (CT - 1)]).astype(BF16)


def body(tile_values, tile_index, keep_rows, slot_place):
    dma = pltpu.SemaphoreType.DMA
    anywhere = pl.BlockSpec(memory_space=pl.ANY)
    scratch = [pltpu.VMEM((SLOTS + 1, TS, TS), BF16)] * (1 + 7 + 7 + 8)
    scratch += [pltpu.SMEM((1, SLOTS), I32), pltpu.SMEM((KEEP, 64), I32), pltpu.SMEM((KEEP, 64), I32)]
    scratch += [pltpu.VMEM((8, 1, TS), I32)] * 3 + [pltpu.SMEM((8, 1, TS), I32)] * 3
    scratch += [
        pltpu.VMEM((2, 1, TS), I32),
        pltpu.SMEM((2, 1, TS), I32),
        pltpu.VMEM((NQ, RT * TS, CT * TS), BF16),
        pltpu.VMEM((NQ, NW, 2 * RT * TS, WIDE), BF16),
        pltpu.VMEM((RT * CT, TS, TS), F32),
        pltpu.VMEM((NROW, CT + 1, 1, TS), F32),
        pltpu.VMEM((NROW, CT + 1, 1, TS), F32),
        pltpu.VMEM((CT, 1, TS), F32),
        pltpu.VMEM((NROW, TS, TS), jnp.int16),
        pltpu.VMEM((NROW, TS, TS), jnp.int16),
    ]
    scratch += [dma((8, MOST))] * 6 + [dma((8,))] * 9 + [dma((NROW,))] * 4 + [dma((5,))]
    return pl.pallas_call(
        kernel,
        out_shape=jax.ShapeDtypeStruct((1, UNITS, TS, TS), BF16),
        in_specs=[anywhere] * 4,
        out_specs=pl.BlockSpec(memory_space=pltpu.VMEM),
        scratch_shapes=scratch,
        compiler_params=pltpu.CompilerParams(collective_id=0, has_side_effects=True, vmem_limit_bytes=56 * 2**20),
        cost_estimate=pl.CostEstimate(flops=2 * 512 * 8192 * 1024, bytes_accessed=2**20, transcendentals=0),
        name="clustering_step",
    )(tile_values, tile_index, keep_rows.T, slot_place.T)


def solution(mesh):
    placed = (P("row", "col", None, None), P("row", "col"), P(), P())
    return jax.shard_map(
        body, mesh=mesh, in_specs=placed, out_specs=P("col", "row", None, None), check_vma=False
    )
```

```python
import jax
import jax.numpy as jnp
from jax import lax
from jax.experimental import pallas as pl
from jax.experimental.pallas import tpu as pltpu
from jax.sharding import PartitionSpec as P

MESH = pl.DeviceIdType.MESH
TS = 128
RT = 4
CT = 8
SLOTS = 16
NROW = 16
NCOL = 8
KEEP = 8
UNITS = 4
NQ = 8
WIDE = 256
NW = CT * TS // WIDE
BATCH = 4
LEVELS = 32767.0
F32 = jnp.float32
I32 = jnp.int32
BF16 = jnp.bfloat16

BEHIND, AHEAD, PARTNER, FAR, BEHIND2, AHEAD2, FAR2, OWN = range(8)
NEAR_PIECES = {
    "+": [(0, 4, "+"), (4, 4, "+"), (8, 4, "+"), (12, 4, "+")],
    "-": [(8, 4, "-"), (12, 4, "-"), (0, 4, "-"), (4, 4, "-")],
    "zb": [(0, 4, "z"), (12, 4, "z"), (4, 4, "z"), (8, 4, "z")],
    "za": [(0, 4, "z"), (12, 4, "z"), (8, 4, "z"), (4, 2, "z"), (6, 2, "z")],
}
FAR_PIECES = [(0, 4, "+"), (4, 4, "+"), (8, 4, "-"), (12, 4, "-")]
FAR2_PIECES = {
    "b": [(0, 4, "+"), (4, 2, "+"), (6, 2, "z"), (8, 2, "z"), (10, 2, "-"), (12, 4, "-")],
    "a": [(0, 4, "+"), (4, 4, "z"), (8, 4, "z"), (12, 4, "-")],
}
PIECES = {
    axis: {
        BEHIND: NEAR_PIECES["+"], AHEAD: NEAR_PIECES["-"], PARTNER: NEAR_PIECES["z" + axis], FAR: FAR_PIECES,
        BEHIND2: [(s, n, "+") for s, n, _ in NEAR_PIECES["z" + axis]], AHEAD2: [(s, n, "-") for s, n, _ in NEAR_PIECES["z" + axis]],
        FAR2: FAR2_PIECES[axis], OWN: [(0, 4, ""), (4, 4, ""), (8, 4, ""), (12, 4, "")],
    }
    for axis in "ab"
}
MOST = 6
PARTNERS = [('b', 0), ('b', 1), ('a', 0), ('b', 2), ('b', 3), ('a', 1), ('a', 2), ('a', 3), ('a', 4)]
HELD = {"b": {(FAR, 0), (FAR, 1), (FAR, 2), (FAR, 3), (FAR2, 0), (FAR2, 1), (FAR2, 4), (FAR2, 5)}, "a": {(FAR2, 0), (FAR2, 3)}}
STEP = {
    "b": {OWN: 0, BEHIND: 1, AHEAD: 1, PARTNER: 2, BEHIND2: 3, AHEAD2: 3, FAR: 4, FAR2: 7},
    "a": {OWN: 0, BEHIND: 1, AHEAD: 1, FAR: 2, PARTNER: 3, BEHIND2: 5, AHEAD2: 5, FAR2: 6},
}
SLICES = {0: 1, 4: 1, 6: 1, 8: 1, 9: 2, 10: 2, 11: 8}


def origin(unit, way):
    if unit in (BEHIND, AHEAD, PARTNER):
        return OWN
    if unit in (BEHIND2, AHEAD2):
        return PARTNER
    if unit == FAR:
        return BEHIND if way == "+" else AHEAD
    return {"+": BEHIND2, "-": AHEAD2, "z": FAR}[way]


def follow_ups(axis, unit, i):
    first, count, _ = PIECES[axis][unit][i]
    found = []
    for nxt in (FAR, BEHIND2, AHEAD2, FAR2):
        for k, (s, n, way) in enumerate(PIECES[axis][nxt]):
            if origin(nxt, way) == unit and first <= s and s + n <= first + count:
                found.append((nxt, k))
    return found


def arrivals():
    free, waiting, done = {}, {}, []
    for axis in "ba":
        for unit in (PARTNER, BEHIND, AHEAD):
            for i, (_, n, way) in enumerate(PIECES[axis][unit]):
                first = PARTNERS.index((axis, i)) if unit == PARTNER else i
                link = way if way == "z" else axis + way
                waiting.setdefault(link, []).append((0.0, first, axis, unit, i, n / 4))
                free[link] = 0.0
    count, held, partner = 100, {"a": [], "b": []}, {"a": 4, "b": 4, "a": 5}
    while any(waiting.values()):
        link = min((n for n in waiting if waiting[n]), key=lambda n: (max(free[n], min(waiting[n])[0]), n))
        item = min(waiting[link], key=lambda m: (max(m[0], free[link]), m[1], m[2]))
        waiting[link].remove(item)
        ready, _, axis, unit, i, cost = item
        free[link] = max(free[link], ready) + cost
        partner[axis] -= unit == PARTNER
        sends = follow_ups(axis, unit, i)
        if partner[axis]:
            held[axis] += [m for m in sends if m in HELD[axis]]
            sends = [m for m in sends if m not in HELD[axis]]
        elif held[axis]:
            sends += sorted(held[axis])
            held[axis] = []
        done.append((free[link], axis, unit, i, sends))
        for nxt, k in sends:
            count += 1
            _, n, way = PIECES[axis][nxt][k]
            waiting[way if way == "z" else axis + way].append((free[link], count, axis, nxt, k, n / 4))
    return sorted(done, key=lambda m: m[0])


def eye_tile():
    rows = lax.broadcasted_iota(I32, (TS, TS), 0)
    cols = lax.broadcasted_iota(I32, (TS, TS), 1)
    return jnp.where(rows == cols, 1.0, 0.0).astype(F32)


def kernel(values, index_in, keep_in, place_in, out, own, *scratch):
    got_a, scratch = scratch[:7], scratch[7:]
    got_b, scratch = scratch[:7], scratch[7:]
    got_s, scratch = scratch[:8], scratch[8:]
    (
        index, keep, place,
        map_a, map_b, map_s, smap_a, smap_b, smap_s, route, sroute,
        dense_a, dense_b, total, sums_out, sums_in, scale, tiles_out, tiles_in,
        send_a, recv_a, send_b, recv_b, send_s, recv_s,
        msend_a, mrecv_a, msend_b, mrecv_b, msend_s, mrecv_s, mlocal_a, mlocal_b, mlocal_s,
        ssend, srecv, tsend, trecv, local,
    ) = scratch

    r = lax.axis_index("row")
    c = lax.axis_index("col")
    core = r % 2
    ring_pos = {"a": c // 2, "b": (r // 2) % 4}
    plane = {"a": c % 2, "b": r // 8}
    got = {"a": got_a, "b": got_b}
    send = {"a": send_a, "b": send_b}
    recv = {"a": recv_a, "b": recv_b}
    maps = {"a": map_a, "b": map_b, "s": map_s}
    smaps = {"a": smap_a, "b": smap_b, "s": smap_s}
    msend = {"a": msend_a, "b": msend_b}
    mrecv = {"a": mrecv_a, "b": mrecv_b}
    mlocal = {"a": mlocal_a, "b": mlocal_b, "s": mlocal_s}
    pending = []

    def block_of(axis, pos, side):
        return pos * 2 + side if axis == "a" else side * 8 + pos * 2 + core

    def device_of(axis, pos, side):
        block = block_of(axis, pos, side)
        return (r, block) if axis == "a" else (block, c)

    def towards(axis, way):
        pos, side = ring_pos[axis], plane[axis]
        if way == "z":
            return device_of(axis, pos, 1 - side)
        return device_of(axis, (pos + (1 if way == "+" else 3)) % 4, side)

    sibling = (r + 1 - 2 * core, c)

    index_copy = pltpu.make_async_copy(index_in, index, local.at[2])
    index_copy.start()
    own_copy = pltpu.make_async_copy(values.at[0], own.at[pl.ds(0, SLOTS)], local.at[0])
    own_copy.start()

    barrier = pltpu.get_barrier_semaphore()
    neighbours = [sibling] + [towards(axis, way) for axis in "ab" for way in "+-z"]
    for device in neighbours:
        pl.semaphore_signal(barrier, inc=1, device_id=device, device_id_type=MESH)
    pl.semaphore_wait(barrier, len(neighbours))

    def remote(src, dst, send_sem, recv_sem, device):
        return pltpu.make_async_remote_copy(
            src_ref=src, dst_ref=dst, send_sem=send_sem, recv_sem=recv_sem, device_id=device, device_id_type=MESH
        )

    def part(ref, piece):
        return ref.at[pl.ds(piece[0], piece[1])]

    def bulk(axis, unit, i):
        piece = PIECES[axis][unit][i]
        source = origin(unit, piece[2])
        src = values.at[0] if source == OWN else got[axis][source]
        return remote(
            part(src, piece), part(got[axis][unit], piece), send[axis].at[unit, i], recv[axis].at[unit, i], towards(axis, piece[2])
        )

    def across(unit, i):
        piece = PIECES["b"][unit][i]
        src = values.at[0] if unit == OWN else got_b[unit]
        return remote(part(src, piece), part(got_s[unit], piece), send_s.at[unit, i], recv_s.at[unit, i], sibling)

    def map_copy(axis, unit):
        way = "z" if unit == PARTNER else "-" if unit in (AHEAD, AHEAD2) else "+"
        ref = maps[axis]
        return remote(ref.at[origin(unit, way)], ref.at[unit], msend[axis].at[unit], mrecv[axis].at[unit], towards(axis, way))

    def map_across(unit):
        return remote(map_b.at[unit], map_s.at[unit], msend_s.at[unit], mrecv_s.at[unit], sibling)

    def map_inward(axis, unit):
        return pltpu.make_async_copy(maps[axis].at[unit], smaps[axis].at[unit], mlocal[axis].at[unit])

    def start_all(*copies):
        for make, *args in copies:
            make(*args).start()
            pending.append((make, *args))

    def pass_map(axis, unit):
        map_copy(axis, unit).wait_recv()
        onward = {BEHIND: [FAR], PARTNER: [BEHIND2, AHEAD2], BEHIND2: [FAR2]}.get(unit, [])
        start_all(*[(map_copy, axis, nxt) for nxt in onward])
        map_inward(axis, unit).start()
        if axis == "b":
            start_all((map_across, unit))

    def start_own(i):
        for axis, k in PARTNERS[2 * i : 2 * i + 2 + (i == 3)]:
            start_all((bulk, axis, PARTNER, k))
        for axis in "ba":
            start_all((bulk, axis, BEHIND, i), (bulk, axis, AHEAD, i))

    start_own(0)
    index_copy.wait()
    lane = lax.broadcasted_iota(I32, (1, TS), 1)
    slot_of = jnp.full((1, TS), SLOTS, I32)
    for s in range(SLOTS):
        slot_of = jnp.where(lane == index[0, s], s, slot_of)
    map_a[OWN] = slot_of
    map_b[OWN] = slot_of
    for axis in "ab":
        start_all(*[(map_copy, axis, unit) for unit in (BEHIND, AHEAD, PARTNER)])
        map_inward(axis, OWN).start()
    start_all((map_across, OWN))
    for i in range(1, 4):
        start_own(i)
    for i in range(4):
        start_all((across, OWN, i))
    list_copies = [pltpu.make_async_copy(keep_in, keep, local.at[3]), pltpu.make_async_copy(place_in, place, local.at[4])]
    for copy in list_copies:
        copy.start()

    total[...] = jnp.zeros_like(total)
    for block in (own, *got_a, *got_b, *got_s):
        block[SLOTS] = jnp.zeros((TS, TS), BF16)
    for copy in list_copies:
        copy.wait()

    def entry(e, carry):
        sending, coming = carry
        kept = keep[e % KEEP, c * CT + e // KEEP]
        slot = place[e % KEEP, c * CT + e // KEEP]
        holder, owner = kept >> 2, slot >> 2
        sending = jnp.where((lane == owner) & (holder == r), (kept & 3) * CT + e // KEEP, sending)
        coming = jnp.where((lane == (slot & 3)) & (owner == r), holder * CT + e // KEEP, coming)
        return sending, coming

    nothing = jnp.zeros((1, TS), I32)
    sending, coming = lax.fori_loop(0, CT * KEEP, entry, (nothing, nothing))
    route[0] = sending
    route[1] = coming
    route_copy = pltpu.make_async_copy(route, sroute, local.at[1])
    route_copy.start()
    own_copy.wait()

    def lay_rows(block, smap, unit, store):
        @pl.loop(0, RT)
        def _(lr):
            for first in range(0, CT, BATCH):
                some = range(first, first + BATCH)
                tiles = [block[smap[unit, 0, lr * CT + lc]] for lc in some]
                for lc, tile in zip(some, tiles):
                    store(lr, lc, tile)

    def lay_a(block, smap, unit, q):
        def store(lr, lc, tile):
            rows = pl.ds(pl.multiple_of(lr * TS, TS), TS)
            dense_a[q, rows, lc * TS : (lc + 1) * TS] = tile

        lay_rows(block, smap, unit, store)

    def lay_b(block, smap, unit, p):
        q, upper = p // 2, p % 2

        def store(lr, lc, tile):
            rows = pl.ds(pl.multiple_of((upper * RT + lr) * TS, TS), TS)
            j = lc % 2
            dense_b[q, lc // 2, rows, j * TS : (j + 1) * TS] = tile

        lay_rows(block, smap, unit, store)

    def position(axis, unit):
        pos, side = ring_pos[axis], plane[axis]
        shift = {OWN: 0, BEHIND: 3, AHEAD: 1, PARTNER: 0, FAR: 2, BEHIND2: 3, AHEAD2: 1, FAR2: 2}[unit]
        other = unit in (PARTNER, BEHIND2, AHEAD2, FAR2)
        return block_of(axis, (pos + shift) % 4, 1 - side if other else side)

    def lay(which, unit):
        if which == "s":
            for i in range(len(PIECES["b"][unit])):
                across(unit, i).wait_recv()
            map_across(unit).wait_recv()
            inward = map_inward("s", unit)
            inward.start()
            inward.wait()
            lay_b(got_s[unit], smap_s, unit, position("b", unit) + 1 - 2 * core)
            return
        block = own if unit == OWN else got[which][unit]
        map_inward(which, unit).wait()
        (lay_a if which == "a" else lay_b)(block, smaps[which], unit, position(which, unit))

    def step_of(axis, pos, side):
        steps = STEP[axis]
        shift = (pos + 4 - ring_pos[axis]) % 4
        same = side == plane[axis]
        first = jnp.where(same, steps[OWN], steps[PARTNER])
        near = jnp.where(same, steps[BEHIND], steps[BEHIND2])
        far = jnp.where(same, steps[FAR], steps[FAR2])
        return jnp.where(shift == 0, first, jnp.where(shift == 2, far, near))

    def add_eyes(q):
        @pl.when(q == r // 2)
        def _():
            for lr in range(RT):
                cols = pl.ds(pl.multiple_of((core * RT + lr) * TS, TS), TS)
                rows = slice(lr * TS, (lr + 1) * TS)
                dense_a[q, rows, cols] = (dense_a[q, rows, cols].astype(F32) + eye_tile()).astype(BF16)

        @pl.when(q == c)
        def _():
            for lc in range(CT):
                j = lc % 2
                at = (q, lc // 2, slice(lc * TS, (lc + 1) * TS), slice(j * TS, (j + 1) * TS))
                dense_b[at] = (dense_b[at].astype(F32) + eye_tile()).astype(BF16)

    def multiply(q):
        add_eyes(q)
        for n in range(NW):
            product = jnp.dot(dense_a[q], dense_b[q, n], preferred_element_type=F32)
            for lr in range(RT):
                for j in range(WIDE // TS):
                    tile = product[lr * TS : (lr + 1) * TS, j * TS : (j + 1) * TS]
                    total[lr * CT + n * (WIDE // TS) + j] += tile

    events = arrivals()
    missing = {(axis, unit): len(PIECES[axis][unit]) for axis in "ab" for unit in range(OWN)}
    for axis in "ab":
        missing[axis, OWN] = 0
    left = [(axis, unit) for step in range(8) for axis in "ab" for unit in STEP[axis] if STEP[axis][unit] == step]
    phases = []
    for when in sorted({0.0} | {event[0] for event in events}):
        now = [event for event in events if event[0] == when]
        for _, axis, unit, _, _ in now:
            missing[axis, unit] -= 1
        lays = []
        while left and not missing[left[0]] and left[0] != ("b", FAR2):
            lays.append(left.pop(0))
        step = max(-1, min([STEP[axis][unit] for axis, unit in left]) - 1)
        if when % 1 and when < 11:
            carried = now
            phases.append([carried, lays, step, 0])
        else:
            phases.append([now, lays, step, SLICES.get(when, 8 if when > 11 else 0)])
    phases.append([[], left, 7, 8])
    merged = []
    for phase in phases:
        if merged and merged[-1][3] == 0:
            before = merged.pop()
            phase = [before[0] + phase[0], before[1] + phase[1], phase[2], phase[3]]
        merged.append(phase)
    phases = merged
    counts = {(axis, unit): len(PIECES[axis][unit]) for axis in "ab" for unit in range(OWN)}

    needs = [jnp.maximum(step_of("a", q // 2, q % 2), step_of("b", q % 4, q // 4)) for q in range(NQ)]
    places = []

    def total_of(terms):
        return sum(terms[1:], terms[0])

    for q in range(NQ):
        before = [(needs[p] <= needs[q] if p < q else needs[p] < needs[q]).astype(I32) for p in range(NQ) if p != q]
        places.append(total_of(before))

    def phase_work(phase):
        for _, axis, unit, k, sends in phase[0]:
            bulk(axis, unit, k).wait_recv()
            start_all(*[(bulk, axis, nxt, kk) for nxt, kk in sends])
            if axis == "b":
                start_all((across, unit, k))
            counts[axis, unit] -= 1
            if counts[axis, unit] == (2 if unit in (BEHIND, PARTNER, BEHIND2) else 0):
                pass_map(axis, unit)
        for axis, unit in phase[1]:
            lay(axis, unit)
            if axis == "b":
                lay("s", unit)

    def one_phase(t, done):
        for i, phase in enumerate(phases):
            pl.when(t == i)(lambda phase=phase: phase_work(phase))
        upto = total_of([(t == i).astype(I32) * phase[2] for i, phase in enumerate(phases)])
        most = total_of([(t == i).astype(I32) * phase[3] for i, phase in enumerate(phases)])
        ready = total_of([(n <= upto).astype(I32) for n in needs])
        until = jnp.maximum(done, jnp.minimum(done + most, ready))

        def one_slice(j, carry):
            q = total_of([(p == j).astype(I32) * i for i, p in enumerate(places)])
            multiply(q)
            return carry

        lax.fori_loop(done, until, one_slice, 0)
        return until

    lax.fori_loop(0, len(phases), one_phase, r * 0)

    route_copy.wait()

    def coded(d):
        e = total[jnp.clip(sroute[0, 0, (r + d) % NROW], 0, RT * CT - 1)]
        top = jnp.max(jnp.abs(e), axis=0, keepdims=True)
        steps_per = jnp.where(top > 0, LEVELS / top, 0.0)
        return jnp.floor(e * steps_per + 0.5).astype(I32).astype(jnp.int16), top

    def tile_move(d):
        return remote(tiles_out.at[d], tiles_in.at[d], tsend.at[d], trecv.at[d], ((r + d) % NROW, c))

    def sums_move(d):
        return remote(sums_out.at[d], sums_in.at[d], ssend.at[d], srecv.at[d], ((r + d) % NROW, c))

    for lc in range(CT):
        column = jnp.zeros((1, TS), F32)
        for lr in range(RT):
            e = total[lr * CT + lc]
            column += jnp.sum(e * e, axis=0, keepdims=True)
        sums_in[0, lc] = column

    @pl.loop(0, NROW - 1)
    def _(i):
        d = NROW // 2 + (i % 2) * ((i + 1) // 2) - (1 - i % 2) * (i // 2)
        tiles_out[d], sums_out[d, CT] = coded(d)
        tile_move(d).start()
        for lc in range(CT):
            sums_out[d, lc] = sums_in[0, lc]
        sums_move(d).start()

    tiles_in[0], sums_in[0, CT] = coded(0)
    for make, *args in pending:
        make(*args).wait_send()

    @pl.loop(1, NROW)
    def _(d):
        sums_move(d).wait()
        tile_move(d).wait()

    for lc in range(CT):
        scale[lc] = float(NROW * RT * TS) / jnp.sum(sums_in[:, lc], axis=0)

    for u in range(UNITS):
        come = sroute[1, 0, u]
        d = jnp.clip((r + NROW - (come >> 3)) % NROW, 0, NROW - 1)
        e = tiles_in[d].astype(I32).astype(F32) * (sums_in[d, CT] * (1.0 / LEVELS))
        out[0, u] = ((e * e) * scale[come & (CT - 1)]).astype(BF16)


def body(tile_values, tile_index, keep_rows, slot_place):
    dma = pltpu.SemaphoreType.DMA
    anywhere = pl.BlockSpec(memory_space=pl.ANY)
    scratch = [pltpu.VMEM((SLOTS + 1, TS, TS), BF16)] * (1 + 7 + 7 + 8)
    scratch += [pltpu.SMEM((1, SLOTS), I32), pltpu.SMEM((KEEP, 64), I32), pltpu.SMEM((KEEP, 64), I32)]
    scratch += [pltpu.VMEM((8, 1, TS), I32)] * 3 + [pltpu.SMEM((8, 1, TS), I32)] * 3
    scratch += [
        pltpu.VMEM((2, 1, TS), I32),
        pltpu.SMEM((2, 1, TS), I32),
        pltpu.VMEM((NQ, RT * TS, CT * TS), BF16),
        pltpu.VMEM((NQ, NW, 2 * RT * TS, WIDE), BF16),
        pltpu.VMEM((RT * CT, TS, TS), F32),
        pltpu.VMEM((NROW, CT + 1, 1, TS), F32),
        pltpu.VMEM((NROW, CT + 1, 1, TS), F32),
        pltpu.VMEM((CT, 1, TS), F32),
        pltpu.VMEM((NROW, TS, TS), jnp.int16),
        pltpu.VMEM((NROW, TS, TS), jnp.int16),
    ]
    scratch += [dma((8, MOST))] * 6 + [dma((8,))] * 9 + [dma((NROW,))] * 4 + [dma((5,))]
    return pl.pallas_call(
        kernel,
        out_shape=jax.ShapeDtypeStruct((1, UNITS, TS, TS), BF16),
        in_specs=[anywhere] * 4,
        out_specs=pl.BlockSpec(memory_space=pltpu.VMEM),
        scratch_shapes=scratch,
        compiler_params=pltpu.CompilerParams(collective_id=0, has_side_effects=True, vmem_limit_bytes=56 * 2**20),
        cost_estimate=pl.CostEstimate(flops=2 * 512 * 8192 * 1024, bytes_accessed=2**20, transcendentals=0),
        name="clustering_step",
    )(tile_values, tile_index, keep_rows.T, slot_place.T)


def solution(mesh):
    placed = (P("row", "col", None, None), P("row", "col"), P(), P())
    return jax.shard_map(
        body, mesh=mesh, in_specs=placed, out_specs=P("col", "row", None, None), check_vma=False
    )
```

```python
import jax
import jax.numpy as jnp
from jax import lax
from jax.experimental import pallas as pl
from jax.experimental.pallas import tpu as pltpu
from jax.sharding import PartitionSpec as P

MESH = pl.DeviceIdType.MESH
TS = 128
RT = 4
CT = 8
SLOTS = 16
NROW = 16
NCOL = 8
KEEP = 8
UNITS = 4
NQ = 8
WIDE = 256
NW = CT * TS // WIDE
BATCH = 8
LEVELS = 32767.0
F32 = jnp.float32
I32 = jnp.int32
BF16 = jnp.bfloat16

BEHIND, AHEAD, PARTNER, FAR, BEHIND2, AHEAD2, FAR2, OWN = range(8)
NEAR_PIECES = {
    "+": [(0, 4, "+"), (4, 4, "+"), (8, 4, "+"), (12, 4, "+")],
    "-": [(8, 4, "-"), (12, 4, "-"), (0, 4, "-"), (4, 4, "-")],
    "zb": [(0, 4, "z"), (12, 4, "z"), (4, 4, "z"), (8, 4, "z")],
    "za": [(0, 4, "z"), (12, 4, "z"), (8, 4, "z"), (4, 2, "z"), (6, 2, "z")],
}
FAR_PIECES = [(0, 4, "+"), (4, 4, "+"), (8, 4, "-"), (12, 4, "-")]
FAR2_PIECES = {
    "b": [(0, 4, "+"), (4, 2, "+"), (6, 2, "z"), (8, 2, "z"), (10, 2, "-"), (12, 4, "-")],
    "a": [(0, 4, "+"), (4, 4, "z"), (8, 4, "z"), (12, 4, "-")],
}
PIECES = {
    axis: {
        BEHIND: NEAR_PIECES["+"], AHEAD: NEAR_PIECES["-"], PARTNER: NEAR_PIECES["z" + axis], FAR: FAR_PIECES,
        BEHIND2: [(s, n, "+") for s, n, _ in NEAR_PIECES["z" + axis]], AHEAD2: [(s, n, "-") for s, n, _ in NEAR_PIECES["z" + axis]],
        FAR2: FAR2_PIECES[axis], OWN: [(0, 4, ""), (4, 4, ""), (8, 4, ""), (12, 4, "")],
    }
    for axis in "ab"
}
MOST = 6
PARTNERS = [('b', 0), ('b', 1), ('a', 0), ('b', 2), ('b', 3), ('a', 1), ('a', 2), ('a', 3), ('a', 4)]
HELD = {"b": {(FAR, 0), (FAR, 1), (FAR, 2), (FAR, 3), (FAR2, 0), (FAR2, 1), (FAR2, 4), (FAR2, 5)}, "a": {(FAR2, 0), (FAR2, 3)}}
STEP = {
    "b": {OWN: 0, BEHIND: 1, AHEAD: 1, PARTNER: 2, BEHIND2: 3, AHEAD2: 3, FAR: 4, FAR2: 7},
    "a": {OWN: 0, BEHIND: 1, AHEAD: 1, FAR: 2, PARTNER: 3, BEHIND2: 5, AHEAD2: 5, FAR2: 6},
}
SLICES = {0: 1, 4: 1, 6: 1, 8: 1, 9: 2, 10: 2, 11: 8}


def origin(unit, way):
    if unit in (BEHIND, AHEAD, PARTNER):
        return OWN
    if unit in (BEHIND2, AHEAD2):
        return PARTNER
    if unit == FAR:
        return BEHIND if way == "+" else AHEAD
    return {"+": BEHIND2, "-": AHEAD2, "z": FAR}[way]


def follow_ups(axis, unit, i):
    first, count, _ = PIECES[axis][unit][i]
    found = []
    for nxt in (FAR, BEHIND2, AHEAD2, FAR2):
        for k, (s, n, way) in enumerate(PIECES[axis][nxt]):
            if origin(nxt, way) == unit and first <= s and s + n <= first + count:
                found.append((nxt, k))
    return found


def arrivals():
    free, waiting, done = {}, {}, []
    for axis in "ba":
        for unit in (PARTNER, BEHIND, AHEAD):
            for i, (_, n, way) in enumerate(PIECES[axis][unit]):
                first = PARTNERS.index((axis, i)) if unit == PARTNER else i
                link = way if way == "z" else axis + way
                waiting.setdefault(link, []).append((0.0, first, axis, unit, i, n / 4))
                free[link] = 0.0
    count, held, partner = 100, {"a": [], "b": []}, {"a": 4, "b": 4, "a": 5}
    while any(waiting.values()):
        link = min((n for n in waiting if waiting[n]), key=lambda n: (max(free[n], min(waiting[n])[0]), n))
        item = min(waiting[link], key=lambda m: (max(m[0], free[link]), m[1], m[2]))
        waiting[link].remove(item)
        ready, _, axis, unit, i, cost = item
        free[link] = max(free[link], ready) + cost
        partner[axis] -= unit == PARTNER
        sends = follow_ups(axis, unit, i)
        if partner[axis]:
            held[axis] += [m for m in sends if m in HELD[axis]]
            sends = [m for m in sends if m not in HELD[axis]]
        elif held[axis]:
            sends += sorted(held[axis])
            held[axis] = []
        done.append((free[link], axis, unit, i, sends))
        for nxt, k in sends:
            count += 1
            _, n, way = PIECES[axis][nxt][k]
            waiting[way if way == "z" else axis + way].append((free[link], count, axis, nxt, k, n / 4))
    return sorted(done, key=lambda m: m[0])


def eye_tile():
    rows = lax.broadcasted_iota(I32, (TS, TS), 0)
    cols = lax.broadcasted_iota(I32, (TS, TS), 1)
    return jnp.where(rows == cols, 1.0, 0.0).astype(F32)


def kernel(values, index_in, keep_in, place_in, out, own, *scratch):
    got_a, scratch = scratch[:7], scratch[7:]
    got_b, scratch = scratch[:7], scratch[7:]
    got_s, scratch = scratch[:8], scratch[8:]
    (
        index, keep, place,
        map_a, map_b, map_s, smap_a, smap_b, smap_s, route, sroute,
        dense_a, dense_b, total, sums_out, sums_in, scale, tiles_out, tiles_in,
        send_a, recv_a, send_b, recv_b, send_s, recv_s,
        msend_a, mrecv_a, msend_b, mrecv_b, msend_s, mrecv_s, mlocal_a, mlocal_b, mlocal_s,
        ssend, srecv, tsend, trecv, local,
    ) = scratch

    r = lax.axis_index("row")
    c = lax.axis_index("col")
    core = r % 2
    ring_pos = {"a": c // 2, "b": (r // 2) % 4}
    plane = {"a": c % 2, "b": r // 8}
    got = {"a": got_a, "b": got_b}
    send = {"a": send_a, "b": send_b}
    recv = {"a": recv_a, "b": recv_b}
    maps = {"a": map_a, "b": map_b, "s": map_s}
    smaps = {"a": smap_a, "b": smap_b, "s": smap_s}
    msend = {"a": msend_a, "b": msend_b}
    mrecv = {"a": mrecv_a, "b": mrecv_b}
    mlocal = {"a": mlocal_a, "b": mlocal_b, "s": mlocal_s}
    pending = []

    def block_of(axis, pos, side):
        return pos * 2 + side if axis == "a" else side * 8 + pos * 2 + core

    def device_of(axis, pos, side):
        block = block_of(axis, pos, side)
        return (r, block) if axis == "a" else (block, c)

    def towards(axis, way):
        pos, side = ring_pos[axis], plane[axis]
        if way == "z":
            return device_of(axis, pos, 1 - side)
        return device_of(axis, (pos + (1 if way == "+" else 3)) % 4, side)

    sibling = (r + 1 - 2 * core, c)

    index_copy = pltpu.make_async_copy(index_in, index, local.at[2])
    index_copy.start()
    own_copy = pltpu.make_async_copy(values.at[0], own.at[pl.ds(0, SLOTS)], local.at[0])
    own_copy.start()

    barrier = pltpu.get_barrier_semaphore()
    neighbours = [sibling] + [towards(axis, way) for axis in "ab" for way in "+-z"]
    for device in neighbours:
        pl.semaphore_signal(barrier, inc=1, device_id=device, device_id_type=MESH)
    pl.semaphore_wait(barrier, len(neighbours))

    def remote(src, dst, send_sem, recv_sem, device):
        return pltpu.make_async_remote_copy(
            src_ref=src, dst_ref=dst, send_sem=send_sem, recv_sem=recv_sem, device_id=device, device_id_type=MESH
        )

    def part(ref, piece):
        return ref.at[pl.ds(piece[0], piece[1])]

    def bulk(axis, unit, i):
        piece = PIECES[axis][unit][i]
        source = origin(unit, piece[2])
        src = values.at[0] if source == OWN else got[axis][source]
        return remote(
            part(src, piece), part(got[axis][unit], piece), send[axis].at[unit, i], recv[axis].at[unit, i], towards(axis, piece[2])
        )

    def across(unit, i):
        piece = PIECES["b"][unit][i]
        src = values.at[0] if unit == OWN else got_b[unit]
        return remote(part(src, piece), part(got_s[unit], piece), send_s.at[unit, i], recv_s.at[unit, i], sibling)

    def map_copy(axis, unit):
        way = "z" if unit == PARTNER else "-" if unit in (AHEAD, AHEAD2) else "+"
        ref = maps[axis]
        return remote(ref.at[origin(unit, way)], ref.at[unit], msend[axis].at[unit], mrecv[axis].at[unit], towards(axis, way))

    def map_across(unit):
        return remote(map_b.at[unit], map_s.at[unit], msend_s.at[unit], mrecv_s.at[unit], sibling)

    def map_inward(axis, unit):
        return pltpu.make_async_copy(maps[axis].at[unit], smaps[axis].at[unit], mlocal[axis].at[unit])

    def start_all(*copies):
        for make, *args in copies:
            make(*args).start()
            pending.append((make, *args))

    def pass_map(axis, unit):
        map_copy(axis, unit).wait_recv()
        onward = {BEHIND: [FAR], PARTNER: [BEHIND2, AHEAD2], BEHIND2: [FAR2]}.get(unit, [])
        start_all(*[(map_copy, axis, nxt) for nxt in onward])
        map_inward(axis, unit).start()
        if axis == "b":
            start_all((map_across, unit))

    def start_own(i):
        for axis, k in PARTNERS[2 * i : 2 * i + 2 + (i == 3)]:
            start_all((bulk, axis, PARTNER, k))
        for axis in "ba":
            start_all((bulk, axis, BEHIND, i), (bulk, axis, AHEAD, i))

    start_own(0)
    index_copy.wait()
    lane = lax.broadcasted_iota(I32, (1, TS), 1)
    slot_of = jnp.full((1, TS), SLOTS, I32)
    for s in range(SLOTS):
        slot_of = jnp.where(lane == index[0, s], s, slot_of)
    map_a[OWN] = slot_of
    map_b[OWN] = slot_of
    for axis in "ab":
        start_all(*[(map_copy, axis, unit) for unit in (BEHIND, AHEAD, PARTNER)])
        map_inward(axis, OWN).start()
    start_all((map_across, OWN))
    for i in range(1, 4):
        start_own(i)
    for i in range(4):
        start_all((across, OWN, i))
    list_copies = [pltpu.make_async_copy(keep_in, keep, local.at[3]), pltpu.make_async_copy(place_in, place, local.at[4])]
    for copy in list_copies:
        copy.start()

    total[...] = jnp.zeros_like(total)
    for block in (own, *got_a, *got_b, *got_s):
        block[SLOTS] = jnp.zeros((TS, TS), BF16)
    for copy in list_copies:
        copy.wait()

    def entry(e, carry):
        sending, coming = carry
        kept = keep[e % KEEP, c * CT + e // KEEP]
        slot = place[e % KEEP, c * CT + e // KEEP]
        holder, owner = kept >> 2, slot >> 2
        sending = jnp.where((lane == owner) & (holder == r), (kept & 3) * CT + e // KEEP, sending)
        coming = jnp.where((lane == (slot & 3)) & (owner == r), holder * CT + e // KEEP, coming)
        return sending, coming

    nothing = jnp.zeros((1, TS), I32)
    sending, coming = lax.fori_loop(0, CT * KEEP, entry, (nothing, nothing))
    route[0] = sending
    route[1] = coming
    route_copy = pltpu.make_async_copy(route, sroute, local.at[1])
    route_copy.start()
    own_copy.wait()

    def lay_rows(block, smap, unit, store):
        @pl.loop(0, RT)
        def _(lr):
            for first in range(0, CT, BATCH):
                some = range(first, first + BATCH)
                tiles = [block[smap[unit, 0, lr * CT + lc]] for lc in some]
                for lc, tile in zip(some, tiles):
                    store(lr, lc, tile)

    def lay_a(block, smap, unit, q):
        def store(lr, lc, tile):
            rows = pl.ds(pl.multiple_of(lr * TS, TS), TS)
            dense_a[q, rows, lc * TS : (lc + 1) * TS] = tile

        lay_rows(block, smap, unit, store)

    def lay_b(block, smap, unit, p):
        q, upper = p // 2, p % 2

        def store(lr, lc, tile):
            rows = pl.ds(pl.multiple_of((upper * RT + lr) * TS, TS), TS)
            j = lc % 2
            dense_b[q, lc // 2, rows, j * TS : (j + 1) * TS] = tile

        lay_rows(block, smap, unit, store)

    def position(axis, unit):
        pos, side = ring_pos[axis], plane[axis]
        shift = {OWN: 0, BEHIND: 3, AHEAD: 1, PARTNER: 0, FAR: 2, BEHIND2: 3, AHEAD2: 1, FAR2: 2}[unit]
        other = unit in (PARTNER, BEHIND2, AHEAD2, FAR2)
        return block_of(axis, (pos + shift) % 4, 1 - side if other else side)

    def lay(which, unit):
        if which == "s":
            for i in range(len(PIECES["b"][unit])):
                across(unit, i).wait_recv()
            map_across(unit).wait_recv()
            inward = map_inward("s", unit)
            inward.start()
            inward.wait()
            lay_b(got_s[unit], smap_s, unit, position("b", unit) + 1 - 2 * core)
            return
        block = own if unit == OWN else got[which][unit]
        map_inward(which, unit).wait()
        (lay_a if which == "a" else lay_b)(block, smaps[which], unit, position(which, unit))

    def step_of(axis, pos, side):
        steps = STEP[axis]
        shift = (pos + 4 - ring_pos[axis]) % 4
        same = side == plane[axis]
        first = jnp.where(same, steps[OWN], steps[PARTNER])
        near = jnp.where(same, steps[BEHIND], steps[BEHIND2])
        far = jnp.where(same, steps[FAR], steps[FAR2])
        return jnp.where(shift == 0, first, jnp.where(shift == 2, far, near))

    def add_eyes(q):
        @pl.when(q == r // 2)
        def _():
            for lr in range(RT):
                cols = pl.ds(pl.multiple_of((core * RT + lr) * TS, TS), TS)
                rows = slice(lr * TS, (lr + 1) * TS)
                dense_a[q, rows, cols] = (dense_a[q, rows, cols].astype(F32) + eye_tile()).astype(BF16)

        @pl.when(q == c)
        def _():
            for lc in range(CT):
                j = lc % 2
                at = (q, lc // 2, slice(lc * TS, (lc + 1) * TS), slice(j * TS, (j + 1) * TS))
                dense_b[at] = (dense_b[at].astype(F32) + eye_tile()).astype(BF16)

    def multiply(q):
        add_eyes(q)
        for n in range(NW):
            product = jnp.dot(dense_a[q], dense_b[q, n], preferred_element_type=F32)
            for lr in range(RT):
                for j in range(WIDE // TS):
                    tile = product[lr * TS : (lr + 1) * TS, j * TS : (j + 1) * TS]
                    total[lr * CT + n * (WIDE // TS) + j] += tile

    events = arrivals()
    missing = {(axis, unit): len(PIECES[axis][unit]) for axis in "ab" for unit in range(OWN)}
    for axis in "ab":
        missing[axis, OWN] = 0
    left = [(axis, unit) for step in range(8) for axis in "ab" for unit in STEP[axis] if STEP[axis][unit] == step]
    phases = []
    for when in sorted({0.0} | {event[0] for event in events}):
        now = [event for event in events if event[0] == when]
        for _, axis, unit, _, _ in now:
            missing[axis, unit] -= 1
        lays = []
        while left and not missing[left[0]] and left[0] != ("b", FAR2):
            lays.append(left.pop(0))
        step = max(-1, min([STEP[axis][unit] for axis, unit in left]) - 1)
        if when % 1 and when < 11:
            carried = now
            phases.append([carried, lays, step, 0])
        else:
            phases.append([now, lays, step, SLICES.get(when, 8 if when > 11 else 0)])
    phases.append([[], left, 7, 8])
    merged = []
    for phase in phases:
        if merged and merged[-1][3] == 0:
            before = merged.pop()
            phase = [before[0] + phase[0], before[1] + phase[1], phase[2], phase[3]]
        merged.append(phase)
    phases = merged
    counts = {(axis, unit): len(PIECES[axis][unit]) for axis in "ab" for unit in range(OWN)}

    needs = [jnp.maximum(step_of("a", q // 2, q % 2), step_of("b", q % 4, q // 4)) for q in range(NQ)]
    places = []

    def total_of(terms):
        return sum(terms[1:], terms[0])

    for q in range(NQ):
        before = [(needs[p] <= needs[q] if p < q else needs[p] < needs[q]).astype(I32) for p in range(NQ) if p != q]
        places.append(total_of(before))

    def phase_work(phase):
        for _, axis, unit, k, sends in phase[0]:
            bulk(axis, unit, k).wait_recv()
            start_all(*[(bulk, axis, nxt, kk) for nxt, kk in sends])
            if axis == "b":
                start_all((across, unit, k))
            counts[axis, unit] -= 1
            if counts[axis, unit] == (2 if unit in (BEHIND, PARTNER, BEHIND2) else 0):
                pass_map(axis, unit)
        for axis, unit in phase[1]:
            lay(axis, unit)
            if axis == "b":
                lay("s", unit)

    def one_phase(t, done):
        for i, phase in enumerate(phases):
            pl.when(t == i)(lambda phase=phase: phase_work(phase))
        upto = total_of([(t == i).astype(I32) * phase[2] for i, phase in enumerate(phases)])
        most = total_of([(t == i).astype(I32) * phase[3] for i, phase in enumerate(phases)])
        ready = total_of([(n <= upto).astype(I32) for n in needs])
        until = jnp.maximum(done, jnp.minimum(done + most, ready))

        def one_slice(j, carry):
            q = total_of([(p == j).astype(I32) * i for i, p in enumerate(places)])
            multiply(q)
            return carry

        lax.fori_loop(done, until, one_slice, 0)
        return until

    lax.fori_loop(0, len(phases), one_phase, r * 0)

    route_copy.wait()

    def coded(d):
        e = total[jnp.clip(sroute[0, 0, (r + d) % NROW], 0, RT * CT - 1)]
        top = jnp.max(jnp.abs(e), axis=0, keepdims=True)
        steps_per = jnp.where(top > 0, LEVELS / top, 0.0)
        return jnp.floor(e * steps_per + 0.5).astype(I32).astype(jnp.int16), top

    def tile_move(d):
        return remote(tiles_out.at[d], tiles_in.at[d], tsend.at[d], trecv.at[d], ((r + d) % NROW, c))

    def sums_move(d):
        return remote(sums_out.at[d], sums_in.at[d], ssend.at[d], srecv.at[d], ((r + d) % NROW, c))

    for lc in range(CT):
        column = jnp.zeros((1, TS), F32)
        for lr in range(RT):
            e = total[lr * CT + lc]
            column += jnp.sum(e * e, axis=0, keepdims=True)
        sums_in[0, lc] = column

    @pl.loop(0, NROW - 1, unroll=5)
    def _(i):
        d = NROW // 2 + (i % 2) * ((i + 1) // 2) - (1 - i % 2) * (i // 2)
        tiles_out[d], sums_out[d, CT] = coded(d)
        tile_move(d).start()
        for lc in range(CT):
            sums_out[d, lc] = sums_in[0, lc]
        sums_move(d).start()

    tiles_in[0], sums_in[0, CT] = coded(0)
    for make, *args in pending:
        make(*args).wait_send()

    @pl.loop(1, NROW)
    def _(d):
        sums_move(d).wait()
        tile_move(d).wait()

    for lc in range(CT):
        scale[lc] = float(NROW * RT * TS) / jnp.sum(sums_in[:, lc], axis=0)

    for u in range(UNITS):
        come = sroute[1, 0, u]
        d = jnp.clip((r + NROW - (come >> 3)) % NROW, 0, NROW - 1)
        e = tiles_in[d].astype(I32).astype(F32) * (sums_in[d, CT] * (1.0 / LEVELS))
        out[0, u] = ((e * e) * scale[come & (CT - 1)]).astype(BF16)


def body(tile_values, tile_index, keep_rows, slot_place):
    dma = pltpu.SemaphoreType.DMA
    anywhere = pl.BlockSpec(memory_space=pl.ANY)
    scratch = [pltpu.VMEM((SLOTS + 1, TS, TS), BF16)] * (1 + 7 + 7 + 8)
    scratch += [pltpu.SMEM((1, SLOTS), I32), pltpu.SMEM((KEEP, 64), I32), pltpu.SMEM((KEEP, 64), I32)]
    scratch += [pltpu.VMEM((8, 1, TS), I32)] * 3 + [pltpu.SMEM((8, 1, TS), I32)] * 3
    scratch += [
        pltpu.VMEM((2, 1, TS), I32),
        pltpu.SMEM((2, 1, TS), I32),
        pltpu.VMEM((NQ, RT * TS, CT * TS), BF16),
        pltpu.VMEM((NQ, NW, 2 * RT * TS, WIDE), BF16),
        pltpu.VMEM((RT * CT, TS, TS), F32),
        pltpu.VMEM((NROW, CT + 1, 1, TS), F32),
        pltpu.VMEM((NROW, CT + 1, 1, TS), F32),
        pltpu.VMEM((CT, 1, TS), F32),
        pltpu.VMEM((NROW, TS, TS), jnp.int16),
        pltpu.VMEM((NROW, TS, TS), jnp.int16),
    ]
    scratch += [dma((8, MOST))] * 6 + [dma((8,))] * 9 + [dma((NROW,))] * 4 + [dma((5,))]
    return pl.pallas_call(
        kernel,
        out_shape=jax.ShapeDtypeStruct((1, UNITS, TS, TS), BF16),
        in_specs=[anywhere] * 4,
        out_specs=pl.BlockSpec(memory_space=pltpu.VMEM),
        scratch_shapes=scratch,
        compiler_params=pltpu.CompilerParams(collective_id=0, has_side_effects=True, vmem_limit_bytes=56 * 2**20),
        cost_estimate=pl.CostEstimate(flops=2 * 512 * 8192 * 1024, bytes_accessed=2**20, transcendentals=0),
        name="clustering_step",
    )(tile_values, tile_index, keep_rows.T, slot_place.T)


def solution(mesh):
    placed = (P("row", "col", None, None), P("row", "col"), P(), P())
    return jax.shard_map(
        body, mesh=mesh, in_specs=placed, out_specs=P("col", "row", None, None), check_vma=False
    )
```
